128 devices in a mesh: wide: 16 (over x, y), narrow: 8 (over z, core).
Axes of the slice: x: 4, y: 4, z: 4, core: 2. Of those that a mesh axis runs over, the one named last changes fastest.
Arguments:
- features: bfloat16 [1024, 64, 512], P(('wide', 'narrow')), may hold values from -6 to 6
- kernel_one: bfloat16 [27, 64, 64], replicated, may hold values from -0.15625 to 0.15625
- kernel_two: bfloat16 [27, 64, 64], replicated, may hold values from -0.15625 to 0.15625
- cotangent: bfloat16 [1024, 64, 512], P(('wide', 'narrow')), may hold values from -6 to 6
- neighbours: int32 [1024, 26], P(('wide', 'narrow')), may hold values from -1 to 1023, as said below
- occupancy: int32 [1024, 512], P(('wide', 'narrow')), may hold values from 0 to 1, as said below
Outputs:
- output: bfloat16 [1024, 64, 512], P(('wide', 'narrow'))
- grad_in: bfloat16 [1024, 64, 512], P(('wide', 'narrow'))
- grad_one: float32 [27, 64, 64], replicated
- grad_two: float32 [27, 64, 64], replicated
The draws below stay inside these ranges and needn't reach their ends.
Inputs may be any that keep to these rules, and one draw needn't show every extreme that they name: neighbours[b, dir] is the global slot (device index along wide then narrow, times 8, plus the slot) of the live brick beside brick b in direction dir, or -1. The lists are symmetric: c stands in direction dir of b exactly when b stands in direction 25 - dir of c. Every neighbour lies on the device of b or on the device just before or just after it in that order. On every device at most 4 bricks have a neighbour on the next device, and at most as many on the previous one; every device but the last has exactly 4 toward the next. A slot that holds no brick lists no neighbours. `occupancy`: A slot that holds no brick has no active voxel.
All inputs are finite; a program needn't handle non-finite values.
Results may differ from the reference program's by a relative error of at most 0.005.
Values may be sent and summed in bfloat16 or wider, within the bound.
No kernel may reach another device: no remote copies, remote signals or barrier semaphores. Data moves between devices by JAX's collectives and lax.ppermute only.
A program may use at most 192 MiB of HBM per device.

```python
import jax
import jax.numpy as jnp
import numpy as np

CH = 64
EDGE = 8
CROSS = 2
SLOTS = 8
VOX = 512
BRICKS = 1024


OFFSETS = [(a, b, c) for a in (-1, 0, 1) for b in (-1, 0, 1) for c in (-1, 0, 1) if (a, b, c) != (0, 0, 0)]


def brick_layout(key):
    folded = jax.random.fold_in(key, 11)
    key_live, key_order, key_voxel = jax.random.split(folded, 3)
    device_count = BRICKS // SLOTS
    depth_count = SLOTS // (CROSS * CROSS)
    positions = jnp.arange(SLOTS, dtype=jnp.int32)
    layer_of = positions // (CROSS * CROSS)
    coin_flip = jax.random.randint(key_live, (device_count, SLOTS), 0, 2)
    live_place = jnp.where(((layer_of == 0) | (layer_of == depth_count - 1))[None, :], 1, coin_flip)
    placement = jax.vmap(lambda k: jax.random.permutation(k, SLOTS))(jax.random.split(key_order, device_count)).astype(jnp.int32)
    slot_of = jnp.argsort(placement, axis=1).astype(jnp.int32)
    live_slot = jnp.take_along_axis(live_place, placement, axis=1)
    device_ids = jnp.arange(device_count, dtype=jnp.int32)[:, None]
    coord_x = device_ids * depth_count + placement // (CROSS * CROSS)
    coord_y = placement // CROSS % CROSS
    coord_z = placement % CROSS
    columns = []
    for a, b, c in OFFSETS:
        near_x = coord_x + a
        near_y = coord_y + b
        near_z = coord_z + c
        inside = (near_x >= 0) & (near_x < device_count * depth_count) & (near_y >= 0) & (near_y < CROSS) & (near_z >= 0) & (near_z < CROSS)
        clip_x = jnp.clip(near_x, 0, device_count * depth_count - 1)
        near_device = clip_x // depth_count
        near_place = clip_x % depth_count * CROSS * CROSS + jnp.clip(near_y, 0, CROSS - 1) * CROSS + jnp.clip(near_z, 0, CROSS - 1)
        near_slot = slot_of[near_device, near_place]
        near_live = live_place[near_device, near_place]
        usable = inside & (live_slot == 1) & (near_live == 1)
        columns.append(jnp.where(usable, near_device * SLOTS + near_slot, -1))
    neighbours = jnp.stack(columns, axis=-1).reshape(BRICKS, 26).astype(jnp.int32)
    voxels = (jax.random.randint(key_voxel, (BRICKS, VOX), 0, 5) < 3).astype(jnp.int32) * live_slot.reshape(BRICKS, 1)
    return (neighbours, voxels.astype(jnp.int32))


def draw_neighbours(key, part):
    return brick_layout(key)[0]


def draw_occupancy(key, part):
    return brick_layout(key)[1]


def shard_levels(key, extent, cuts, least, largest):
    loudness, own = 1.0, jax.random.fold_in(key, 6)
    for position, parts in cuts:
        steps = jnp.exp(jax.random.uniform(jax.random.fold_in(own, position), (parts,), jnp.float32, least / len(cuts), largest / len(cuts)))
        loudness = loudness * jnp.repeat(steps, extent[position] // parts).reshape([-1 if axis == position else 1 for axis in range(len(extent))])
    return loudness


def centred(stream_key, extent, scale, limit, cuts=(), held_as=jnp.bfloat16):
    gain = shard_levels(stream_key, extent, cuts, -0.22, 0.18) if cuts else 1.0
    array = jax.random.normal(stream_key, extent, jnp.float32) * scale * gain
    return jnp.minimum(jnp.maximum(array, -limit), limit).astype(held_as)


def setup_inputs(seed: int = 0) -> dict:
    key_list = jax.random.split(jax.random.key(seed), 7)
    return {
        "features": centred(key_list[0], (BRICKS, CH, VOX), 1.0, 6.0, ((0, 128),)),
        "kernel_one": centred(key_list[1], (27, CH, CH), (27 * CH) ** -0.5, 0.15625),
        "kernel_two": centred(key_list[2], (27, CH, CH), (27 * CH) ** -0.5, 0.15625),
        "cotangent": centred(key_list[3], (BRICKS, CH, VOX), 1.0, 6.0, ((0, 128),)),
        "neighbours": draw_neighbours(jax.random.fold_in(key_list[6], 71), 0),
        "occupancy": draw_occupancy(jax.random.fold_in(key_list[6], 71), 0),
    }


def offset_tables(edge):
    cell_ids = np.arange(edge ** 3)
    first = cell_ids // (edge * edge)
    second = cell_ids // edge % edge
    third = cell_ids % edge
    direction_codes = []
    source_cells = []
    for a in range(3):
        for b in range(3):
            for c in range(3):
                shifted_ids = [first + a - 1, second + b - 1, third + c - 1]
                side_codes = [(m >= edge).astype(np.int64) - (m < 0).astype(np.int64) for m in shifted_ids]
                direction_codes.append((side_codes[0] + 1) * 9 + (side_codes[1] + 1) * 3 + side_codes[2] + 1)
                wrapped = [m % edge for m in shifted_ids]
                source_cells.append((wrapped[0] * edge + wrapped[1]) * edge + wrapped[2])
    return (np.stack(direction_codes).astype(np.int32), np.stack(source_cells).astype(np.int32))

def gather_index(lookup, usable, zero_at):
    brick_count = lookup.shape[0]
    direction_codes, source_cells = offset_tables(EDGE)
    own_slots = jnp.arange(brick_count, dtype=jnp.int32)[:, None]
    lookup_full = jnp.concatenate([lookup[:, :13], own_slots, lookup[:, 13:]], axis=1).astype(jnp.int32)
    usable_full = jnp.concatenate([usable[:, :13], jnp.ones((brick_count, 1), bool), usable[:, 13:]], axis=1)
    brick_ids = jnp.take(lookup_full, jnp.asarray(direction_codes), axis=1)
    present = jnp.take(usable_full, jnp.asarray(direction_codes), axis=1)
    gather_rows = jnp.where(present, brick_ids * VOX + jnp.asarray(source_cells)[None], zero_at)
    return gather_rows.transpose(1, 0, 2).reshape(27, -1).astype(jnp.int32)

def flatten(volume):
    return volume.transpose(1, 0, 2).reshape(volume.shape[1], -1)

def unflatten(flattened, brick_count):
    return flattened.reshape(flattened.shape[0], brick_count, -1).transpose(1, 0, 2)

def with_zeros(flattened):
    return jnp.concatenate([flattened, jnp.zeros((flattened.shape[0], VOX), flattened.dtype)], axis=1)

def convolve(pool_flat, gather_rows, weights):
    accumulated = None
    for group in range(9):
        shifted = jnp.take(pool_flat, gather_rows[3 * group:3 * group + 3], axis=1).astype(jnp.float32)
        summand = jnp.einsum('qcm,cpq->pm', shifted, weights[3 * group:3 * group + 3].astype(jnp.float32))
        accumulated = summand if accumulated is None else accumulated + summand
    return accumulated

def kernel_grad(pool_flat, gather_rows, grad_flat):
    pieces = []
    grad_wide = grad_flat.astype(jnp.float32)
    for group in range(9):
        shifted = jnp.take(pool_flat, gather_rows[3 * group:3 * group + 3], axis=1).astype(jnp.float32)
        pieces.append(jnp.einsum('pm,qcm->cpq', grad_wide, shifted))
    return jnp.concatenate(pieces, axis=0)

def flipped(weights):
    return jnp.flip(weights, 0).transpose(0, 2, 1)

def reference(features, kernel_one, kernel_two, cotangent, neighbours, occupancy):
    bricks = features.shape[0]
    active = occupancy.astype(jnp.bfloat16)[:, None, :]
    mask_flat = occupancy.astype(jnp.float32).reshape(1, -1)
    usable = neighbours >= 0
    lookup = jnp.maximum(neighbours, 0).astype(jnp.int32)
    gather_rows = gather_index(lookup, usable, bricks * VOX)
    inputs = with_zeros(flatten(features * active))
    preact = convolve(inputs, gather_rows, kernel_one)
    hidden = with_zeros((jax.nn.silu(preact) * mask_flat).astype(jnp.bfloat16))
    output = (convolve(hidden, gather_rows, kernel_two) * mask_flat).astype(jnp.bfloat16)
    grad_out_flat = flatten(cotangent * active)
    back_two = convolve(with_zeros(grad_out_flat), gather_rows, flipped(kernel_two))
    sigmoid_pre = jax.nn.sigmoid(preact)
    grad_pre = (back_two * sigmoid_pre * (1.0 + preact * (1.0 - sigmoid_pre)) * mask_flat).astype(jnp.bfloat16)
    grad_in = (convolve(with_zeros(grad_pre), gather_rows, flipped(kernel_one)) * mask_flat).astype(jnp.bfloat16)
    normalizer = 1.0 / jnp.sqrt(jnp.float32(BRICKS * VOX))
    grad_one = kernel_grad(inputs, gather_rows, grad_pre) * normalizer
    grad_two = kernel_grad(hidden, gather_rows, grad_out_flat) * normalizer
    return (unflatten(output, bricks), unflatten(grad_in, bricks), grad_one, grad_two)
```

```python
import jax
import jax.numpy as jnp
from jax import lax
from jax.experimental import pallas as pl
from jax.experimental.pallas import tpu as pltpu
from jax.sharding import PartitionSpec as P

AXES = ("wide", "narrow")
SLOTS = 8
EDGE = 8
VOX = EDGE**3
CH = 64
LANES = 2 * CH
NEAR = 4
POOL = SLOTS + 2 * NEAR + 1
ZERO = POOL - 1
SLAB = (EDGE + 2) * EDGE
TILE_ROWS = (EDGE + 2) * SLAB
ROWS = EDGE * SLAB
TERMS = 2048
VMEM = 48 * 1024 * 1024
F32 = jnp.float32
BF16 = jnp.bfloat16

whole_vmem = pl.BlockSpec(memory_space=pltpu.VMEM)
whole_smem = pl.BlockSpec(memory_space=pltpu.SMEM)
anywhere = pl.BlockSpec(memory_space=pl.ANY)


def lower_half(shape):
    return lax.broadcasted_iota(jnp.int32, shape, len(shape) - 1) < CH


def pack_kernel(position, neighbours, features, cotangent, occupancy, fields, ahead, behind, chosen):
    for b in range(SLOTS):
        active = occupancy[b : b + 1, :].astype(F32)
        both = jnp.concatenate([features[b], cotangent[b]], axis=0).astype(F32) * active
        fields[b] = both.T.astype(BF16)
    here = position[0] * SLOTS
    for r in range(SLOTS):
        chosen[0, r] = 0
        chosen[1, r] = 0
    count_ahead = jnp.int32(0)
    count_behind = jnp.int32(0)
    for b in range(SLOTS):
        highest = jnp.int32(-1)
        lowest = jnp.int32(1 << 20)
        for d in range(26):
            slot = neighbours[b, d]
            highest = jnp.maximum(highest, slot)
            lowest = jnp.minimum(lowest, jnp.where(slot < 0, 1 << 20, slot))
        chosen[0, jnp.minimum(count_ahead, NEAR)] = b
        chosen[1, jnp.minimum(count_behind, NEAR)] = b
        count_ahead += (highest >= here + SLOTS).astype(jnp.int32)
        count_behind += (lowest < here).astype(jnp.int32)
    for r in range(NEAR):
        ahead[r] = fields[chosen[0, r]]
        behind[r] = fields[chosen[1, r]]


def pack(position, neighbours, features, cotangent, occupancy):
    return pl.pallas_call(
        pack_kernel,
        out_shape=(
            jax.ShapeDtypeStruct((SLOTS, VOX, LANES), BF16),
            jax.ShapeDtypeStruct((NEAR, VOX, LANES), BF16),
            jax.ShapeDtypeStruct((NEAR, VOX, LANES), BF16),
            jax.ShapeDtypeStruct((2, SLOTS), jnp.int32),
        ),
        in_specs=[whole_smem, whole_smem, whole_vmem, whole_vmem, whole_vmem],
        out_specs=(whole_vmem, whole_vmem, whole_vmem, whole_smem),
        compiler_params=pltpu.CompilerParams(vmem_limit_bytes=VMEM),
        name="pack",
    )(position, neighbours, features, cotangent, occupancy)


def weight_block(kernel, flip, a, rows, columns):
    def piece(c, e):
        if c is None or e is None:
            return jnp.zeros((CH, CH), F32)
        n = 9 * a + 3 * c + e
        return kernel[26 - n if flip else n].astype(F32)

    if flip:
        block = jnp.concatenate(
            [jnp.concatenate([piece(c, e) for c in columns], axis=1) for e in rows], axis=0
        )
    else:
        block = jnp.concatenate(
            [jnp.concatenate([piece(c, e) for e in rows], axis=1) for c in columns], axis=0
        ).T
    return block.astype(BF16)


def weight_field(kernel, flip, field, target):
    rows = ((0, 1), (2, None)) if field == 0 else ((None, 2), (0, 1))
    columns = ((0, 1), (2, None)) if field == 0 else ((1, 0), (None, 2))
    for a in range(3):
        for r in range(2):
            for s in range(2):
                target[
                    field, a, r * LANES : (r + 1) * LANES, s * LANES : (s + 1) * LANES
                ] = weight_block(kernel, flip, a, rows[r], columns[s])


def prepare_kernel(position, neighbours, kernel_one, kernel_two, first, second, lookup, flags, base):
    weight_field(kernel_one, False, 0, first)
    weight_field(kernel_two, True, 1, first)
    weight_field(kernel_two, False, 0, second)
    weight_field(kernel_one, True, 1, second)
    start = (position[0] - 1) * SLOTS
    for s in range(3 * SLOTS + 1):
        flags[s] = 0
    for b in range(SLOTS):
        for d in range(26):
            slot = neighbours[b, d]
            flags[jnp.where(slot < 0, 3 * SLOTS, slot - start)] = 1
    count = jnp.int32(0)
    for s in range(SLOTS):
        base[s] = SLOTS + jnp.minimum(count, NEAR - 1)
        count += flags[s]
        base[SLOTS + s] = s
    count = jnp.int32(0)
    for s in range(SLOTS):
        base[2 * SLOTS + s] = SLOTS + NEAR + jnp.minimum(count, NEAR - 1)
        count += flags[2 * SLOTS + s]
    base[3 * SLOTS] = ZERO
    for b in range(SLOTS):
        lookup[b * 27 + 13] = b
        for d in range(26):
            slot = neighbours[b, d]
            lookup[b * 27 + d + (d > 12)] = base[jnp.where(slot < 0, 3 * SLOTS, slot - start)]


def prepare(position, neighbours, kernel_one, kernel_two):
    return pl.pallas_call(
        prepare_kernel,
        out_shape=(
            jax.ShapeDtypeStruct((2, 3, 2 * LANES, 2 * LANES), BF16),
            jax.ShapeDtypeStruct((2, 3, 2 * LANES, 2 * LANES), BF16),
            jax.ShapeDtypeStruct((27 * SLOTS,), jnp.int32),
        ),
        in_specs=[whole_smem, whole_smem, whole_vmem, whole_vmem],
        out_specs=(whole_vmem, whole_vmem, whole_smem),
        scratch_shapes=[pltpu.SMEM((32,), jnp.int32), pltpu.SMEM((32,), jnp.int32)],
        compiler_params=pltpu.CompilerParams(vmem_limit_bytes=VMEM),
        cost_estimate=pl.CostEstimate(flops=4000000, bytes_accessed=2000000, transcendentals=0),
        name="prepare",
    )(position, neighbours, kernel_one, kernel_two)


def fill_pool(own, before, after, pool, sems):
    copies = [
        pltpu.make_async_copy(own, pool.at[pl.ds(0, SLOTS)], sems.at[0]),
        pltpu.make_async_copy(before, pool.at[pl.ds(SLOTS, NEAR)], sems.at[1]),
        pltpu.make_async_copy(after, pool.at[pl.ds(SLOTS + NEAR, NEAR)], sems.at[2]),
    ]
    for copy in copies:
        copy.start()
    pool[ZERO] = jnp.zeros((VOX, LANES), BF16)
    for copy in copies:
        copy.wait()


def extend(pool, lookup, b, tile):
    def slabs(bricks, first, count):
        return [
            pool[brick, first : first + count, :].astype(F32).reshape(count // EDGE, EDGE, LANES)
            for brick in bricks
        ]

    for i in range(EDGE + 2):
        side = (i + EDGE - 1) // EDGE
        source = (i - 1) % EDGE
        bricks = [
            [lookup[b * 27 + side * 9 + j * 3 + k] for k in range(3)] for j in range(3)
        ]
        left = slabs(bricks[0], source * 64 + 48, 16)
        middle = slabs(bricks[1], source * 64, 64)
        right = slabs(bricks[2], source * 64, 16)
        low, centre, high = [
            jnp.concatenate([left[k][1:2], middle[k], right[k][0:1]], axis=0) for k in range(3)
        ]
        along = lax.broadcasted_iota(jnp.int32, centre.shape, 1)
        first = pltpu.roll(jnp.where(along == EDGE - 1, low, centre), 1, 1)
        last = pltpu.roll(jnp.where(along == 0, high, centre), EDGE - 1, 1)
        first, centre, last = [m.reshape(SLAB, LANES) for m in (first, centre, last)]
        lower = lower_half((SLAB, LANES))
        crossed = pltpu.roll(jnp.where(lower, centre, first), CH, 1)
        rows = pl.ds(i * SLAB, SLAB)
        tile[rows, 0:LANES] = jnp.where(lower, first, crossed).astype(BF16)
        tile[rows, LANES : 2 * LANES] = last.astype(BF16)
        tile[rows, 2 * LANES : 3 * LANES] = jnp.where(lower, crossed, centre).astype(BF16)


def convolve(tile, weights):
    sums = []
    for field in range(2):
        total = None
        for a in range(3):
            part = jnp.dot(
                tile[a * SLAB : a * SLAB + ROWS, field * LANES : (field + 2) * LANES],
                weights[field, a],
                preferred_element_type=F32,
            )
            total = part if total is None else total + part
        sums.append(total)

    def block(field, half):
        return sums[field][:, half * LANES : (half + 1) * LANES].reshape(
            EDGE, EDGE + 2, EDGE, LANES
        )

    zero, one = block(0, 0), block(1, 0)
    shape = (EDGE, EDGE, EDGE, LANES)
    lower = lower_half(shape)
    straight = jnp.where(lower, zero[:, 0:8], one[:, 0:8])
    crossed = jnp.where(lower, one[:, 1:9], zero[:, 1:9]).reshape(VOX, LANES)
    ends = block(0, 1)[:, 2:10] + block(1, 1)[:, 2:10]
    return (straight + ends).reshape(VOX, LANES) + pltpu.roll(crossed, CH, 1)


def row_mask(occupancy, b):
    active = occupancy[pl.ds(b, 1), :].astype(F32)
    return jnp.broadcast_to(active, (LANES, VOX)).T


def first_kernel(
    lookup, chosen, occupancy, weights, own, before, after,
    result, ahead, behind, terms, pool, tile, sum_one, sum_two, sems,
):
    fill_pool(own, before, after, pool, sems)
    sum_one[...] = jnp.zeros_like(sum_one)
    sum_two[...] = jnp.zeros_like(sum_two)

    @pl.loop(0, SLOTS)
    def _(b):
        extend(pool, lookup, b, tile)
        both = convolve(tile, weights)
        lower = lower_half((VOX, LANES))
        preact = jnp.where(lower, both, pltpu.roll(both, CH, 1))
        s = jax.nn.sigmoid(preact)
        value = jnp.where(lower, preact * s, both * s * (1.0 + preact * (1.0 - s)))
        value = value * row_mask(occupancy, b)
        result[b] = value.astype(BF16)
        cube = value.reshape(EDGE, EDGE, EDGE, LANES)
        turned = []
        for c in range(3):
            parts = [cube]
            if c > 0:
                parts.insert(0, jnp.zeros((EDGE, c, EDGE, LANES), F32))
            if c < 2:
                parts.append(jnp.zeros((EDGE, 2 - c, EDGE, LANES), F32))
            padded = jnp.concatenate(parts, axis=1).reshape(ROWS, LANES)
            turned.append(padded.astype(BF16).T)
        hidden = jnp.concatenate([t[:CH] for t in turned], axis=0)
        grad_pre = jnp.concatenate([t[CH:] for t in turned], axis=0)
        for a in range(3):
            rows = pl.ds(a * SLAB, ROWS)
            sum_one[a] += jnp.dot(
                grad_pre, tile[rows, 0 : 2 * LANES], preferred_element_type=F32
            )
            sum_two[a] += jnp.dot(
                hidden, tile[rows, LANES : 3 * LANES], preferred_element_type=F32
            )

    for r in range(NEAR):
        ahead[r] = result[chosen[0, r]]
        behind[r] = result[chosen[1, r]]
    part = 3 * CH
    for a in range(3):
        start = a * 3 * part
        terms[start : start + part] = sum_one[a, :, 0:LANES].astype(BF16)
        terms[start + part : start + 2 * part] = sum_two[a, :, LANES:].astype(BF16)
        terms[start + 2 * part : start + 3 * part] = jnp.where(
            lower_half((part, LANES)), sum_one[a, :, LANES:], sum_two[a, :, 0:LANES]
        ).astype(BF16)
    terms[9 * part :] = jnp.zeros((TERMS - 9 * part, LANES), BF16)


def first_stage(lookup, chosen, occupancy, weights, own, before, after):
    return pl.pallas_call(
        first_kernel,
        out_shape=(
            jax.ShapeDtypeStruct((SLOTS, VOX, LANES), BF16),
            jax.ShapeDtypeStruct((NEAR, VOX, LANES), BF16),
            jax.ShapeDtypeStruct((NEAR, VOX, LANES), BF16),
            jax.ShapeDtypeStruct((TERMS, LANES), BF16),
        ),
        in_specs=[whole_smem, whole_smem, whole_vmem, whole_vmem, anywhere, anywhere, anywhere],
        out_specs=(whole_vmem,) * 4,
        scratch_shapes=[
            pltpu.VMEM((POOL, VOX, LANES), BF16),
            pltpu.VMEM((TILE_ROWS, 3 * LANES), BF16),
            pltpu.VMEM((3, 3 * CH, 2 * LANES), F32),
            pltpu.VMEM((3, 3 * CH, 2 * LANES), F32),
            pltpu.SemaphoreType.DMA((3,)),
        ],
        compiler_params=pltpu.CompilerParams(vmem_limit_bytes=VMEM),
        cost_estimate=pl.CostEstimate(
            flops=8000000000, bytes_accessed=6000000, transcendentals=600000
        ),
        name="first_stage",
    )(lookup, chosen, occupancy, weights, own, before, after)


def second_kernel(
    lookup, occupancy, weights, own, before, after, output, grad_in, pool, tile, sems
):
    fill_pool(own, before, after, pool, sems)

    @pl.loop(0, SLOTS)
    def _(b):
        extend(pool, lookup, b, tile)
        both = convolve(tile, weights).T * occupancy[pl.ds(b, 1), :].astype(F32)
        output[b] = both[:CH].astype(BF16)
        grad_in[b] = both[CH:].astype(BF16)


def second_stage(lookup, occupancy, weights, own, before, after):
    return pl.pallas_call(
        second_kernel,
        out_shape=(
            jax.ShapeDtypeStruct((SLOTS, CH, VOX), BF16),
            jax.ShapeDtypeStruct((SLOTS, CH, VOX), BF16),
        ),
        in_specs=[whole_smem, whole_vmem, whole_vmem, anywhere, anywhere, anywhere],
        out_specs=(whole_vmem,) * 2,
        scratch_shapes=[
            pltpu.VMEM((POOL, VOX, LANES), BF16),
            pltpu.VMEM((TILE_ROWS, 3 * LANES), BF16),
            pltpu.SemaphoreType.DMA((3,)),
        ],
        compiler_params=pltpu.CompilerParams(vmem_limit_bytes=VMEM),
        cost_estimate=pl.CostEstimate(
            flops=8000000000, bytes_accessed=6000000, transcendentals=0
        ),
        name="second_stage",
    )(lookup, occupancy, weights, own, before, after)


def combine_kernel(blocks, spread):
    count, rows = blocks.shape[0], blocks.shape[1]
    total = jnp.zeros((rows, LANES), F32)
    for d in range(count):
        total += blocks[d].astype(F32)
    spread[...] = jnp.broadcast_to(total.astype(BF16)[None], spread.shape)


def combine(blocks):
    return pl.pallas_call(
        combine_kernel,
        out_shape=jax.ShapeDtypeStruct(blocks.shape, BF16),
        in_specs=[whole_vmem],
        out_specs=whole_vmem,
        name="combine",
    )(blocks)


def unpack_kernel(scale, sums, grad_one, grad_two):
    part = 3 * CH
    for a in range(3):
        for c in range(3):
            start = a * 3 * part + c * CH
            n = 9 * a + 3 * c

            def block(which):
                return sums[start + which * part : start + which * part + CH].astype(F32) * scale

            one, two, last = block(0), block(1).T, block(2)
            grad_one[n] = one[:, :CH]
            grad_one[n + 1] = one[:, CH:]
            grad_one[n + 2] = last[:, :CH]
            grad_two[26 - n] = two[:CH]
            grad_two[25 - n] = two[CH:]
            grad_two[24 - n] = last.T[CH:]


def unpack(scale, sums):
    def kernel(*refs):
        unpack_kernel(scale, *refs)

    return pl.pallas_call(
        kernel,
        out_shape=(
            jax.ShapeDtypeStruct((27, CH, CH), F32),
            jax.ShapeDtypeStruct((27, CH, CH), F32),
        ),
        in_specs=[whole_vmem],
        out_specs=(whole_vmem,) * 2,
        name="unpack",
    )(sums)


def exchange(ahead, behind, devices):
    before = lax.ppermute(ahead, AXES, [(k, k + 1) for k in range(devices - 1)])
    after = lax.ppermute(behind, AXES, [(k + 1, k) for k in range(devices - 1)])
    return before, after


def local(devices, features, kernel_one, kernel_two, cotangent, neighbours, occupancy):
    position = lax.axis_index(AXES).astype(jnp.int32).reshape(1)
    fields, ahead, behind, chosen = pack(position, neighbours, features, cotangent, occupancy)
    before, after = exchange(ahead, behind, devices)
    first, second, lookup = prepare(position, neighbours, kernel_one, kernel_two)
    result, ahead, behind, terms = first_stage(
        lookup, chosen, occupancy, first, fields, before, after
    )
    before, after = exchange(ahead, behind, devices)
    terms = lax.all_to_all(terms, AXES, 0, 0, tiled=True)
    output, grad_in = second_stage(lookup, occupancy, second, result, before, after)
    spread = combine(terms.reshape(devices, TERMS // devices, LANES)).reshape(TERMS, LANES)
    sums = lax.all_to_all(spread, AXES, 0, 0, tiled=True)
    scale = float((SLOTS * VOX * devices) ** -0.5)
    grad_one, grad_two = unpack(scale, sums)
    return output, grad_in, grad_one, grad_two


def solution(mesh):
    devices = mesh.shape["wide"] * mesh.shape["narrow"]
    bricks = P(AXES, None, None)
    in_specs = (bricks, P(), P(), bricks, P(AXES, None), P(AXES, None))
    out_specs = (bricks, bricks, P(), P())

    def run(*arrays):
        return local(devices, *arrays)

    return jax.shard_map(
        run, mesh=mesh, in_specs=in_specs, out_specs=out_specs, check_vma=False
    )
```

```python
import jax
import jax.numpy as jnp
from jax import lax
from jax.experimental import pallas as pl
from jax.experimental.pallas import tpu as pltpu
from jax.sharding import PartitionSpec as P

AXES = ("wide", "narrow")
SLOTS = 8
EDGE = 8
VOX = EDGE**3
CH = 64
LANES = 2 * CH
NEAR = 4
POOL = SLOTS + 2 * NEAR + 1
ZERO = POOL - 1
SLAB = (EDGE + 2) * EDGE
TILE_ROWS = (EDGE + 2) * SLAB
ROWS = EDGE * SLAB
TERMS = 2048
VMEM = 24 * 1024 * 1024
F32 = jnp.float32
BF16 = jnp.bfloat16

whole_vmem = pl.BlockSpec(memory_space=pltpu.VMEM)
whole_smem = pl.BlockSpec(memory_space=pltpu.SMEM)
anywhere = pl.BlockSpec(memory_space=pl.ANY)


def lower_half(shape):
    return lax.broadcasted_iota(jnp.int32, shape, len(shape) - 1) < CH


def pack_kernel(
    position, neighbours, features_far, cotangent_far, occupancy_far,
    fields, ahead, behind, chosen, features, cotangent, occupancy, sems,
):
    mask_copy = pltpu.make_async_copy(occupancy_far, occupancy, sems.at[0, 0])
    mask_copy.start()
    copies = []
    for b in range(SLOTS):
        copies.append(
            (
                pltpu.make_async_copy(features_far.at[b], features.at[b], sems.at[1, b]),
                pltpu.make_async_copy(cotangent_far.at[b], cotangent.at[b], sems.at[2, b]),
            )
        )
        for copy in copies[-1]:
            copy.start()
    here = position[0] * SLOTS
    for r in range(SLOTS):
        chosen[0, r] = 0
        chosen[1, r] = 0
    count_ahead = jnp.int32(0)
    count_behind = jnp.int32(0)
    for b in range(SLOTS):
        highest = jnp.int32(-1)
        lowest = jnp.int32(1 << 20)
        for d in range(26):
            slot = neighbours[b, d]
            highest = jnp.maximum(highest, slot)
            lowest = jnp.minimum(lowest, jnp.where(slot < 0, 1 << 20, slot))
        chosen[0, jnp.minimum(count_ahead, NEAR)] = b
        chosen[1, jnp.minimum(count_behind, NEAR)] = b
        count_ahead += (highest >= here + SLOTS).astype(jnp.int32)
        count_behind += (lowest < here).astype(jnp.int32)
    mask_copy.wait()
    for b in range(SLOTS):
        for copy in copies[b]:
            copy.wait()
        active = occupancy[b : b + 1, :].astype(F32)
        both = jnp.concatenate([features[b], cotangent[b]], axis=0).astype(F32) * active
        fields[b] = both.T.astype(BF16)
    for r in range(NEAR):
        ahead[r] = fields[chosen[0, r]]
        behind[r] = fields[chosen[1, r]]


def pack(position, neighbours, features, cotangent, occupancy):
    return pl.pallas_call(
        pack_kernel,
        out_shape=(
            jax.ShapeDtypeStruct((SLOTS, VOX, LANES), BF16),
            jax.ShapeDtypeStruct((NEAR, VOX, LANES), BF16),
            jax.ShapeDtypeStruct((NEAR, VOX, LANES), BF16),
            jax.ShapeDtypeStruct((2, SLOTS), jnp.int32),
        ),
        in_specs=[whole_smem, whole_smem, anywhere, anywhere, anywhere],
        out_specs=(whole_vmem, whole_vmem, whole_vmem, whole_smem),
        scratch_shapes=[
            pltpu.VMEM((SLOTS, CH, VOX), BF16),
            pltpu.VMEM((SLOTS, CH, VOX), BF16),
            pltpu.VMEM((SLOTS, VOX), jnp.int32),
            pltpu.SemaphoreType.DMA((3, SLOTS)),
        ],
        compiler_params=pltpu.CompilerParams(vmem_limit_bytes=60 * 1024 * 1024),
        name="pack",
    )(position, neighbours, features, cotangent, occupancy)


def weight_block(kernel, flip, a, rows, columns):
    def piece(c, e):
        if c is None or e is None:
            return jnp.zeros((CH, CH), F32)
        n = 9 * a + 3 * c + e
        return kernel[26 - n if flip else n].astype(F32)

    if flip:
        block = jnp.concatenate(
            [jnp.concatenate([piece(c, e) for c in columns], axis=1) for e in rows], axis=0
        )
    else:
        block = jnp.concatenate(
            [jnp.concatenate([piece(c, e) for e in rows], axis=1) for c in columns], axis=0
        ).T
    return block.astype(BF16)


def weight_field(kernel, flip, field, target):
    rows = ((0, 1), (2, None)) if field == 0 else ((None, 2), (0, 1))
    columns = ((0, 1), (2, None)) if field == 0 else ((1, 0), (None, 2))
    for a in range(3):
        for r in range(2):
            for s in range(2):
                target[
                    field, a, r * LANES : (r + 1) * LANES, s * LANES : (s + 1) * LANES
                ] = weight_block(kernel, flip, a, rows[r], columns[s])


def prepare_kernel(position, neighbours, kernel_one, kernel_two, first, second, lookup, flags, base):
    weight_field(kernel_one, False, 0, first)
    weight_field(kernel_two, True, 1, first)
    weight_field(kernel_two, False, 0, second)
    weight_field(kernel_one, True, 1, second)
    start = (position[0] - 1) * SLOTS
    for s in range(3 * SLOTS + 1):
        flags[s] = 0
    for b in range(SLOTS):
        for d in range(26):
            slot = neighbours[b, d]
            flags[jnp.where(slot < 0, 3 * SLOTS, slot - start)] = 1
    count = jnp.int32(0)
    for s in range(SLOTS):
        base[s] = SLOTS + jnp.minimum(count, NEAR - 1)
        count += flags[s]
        base[SLOTS + s] = s
    count = jnp.int32(0)
    for s in range(SLOTS):
        base[2 * SLOTS + s] = SLOTS + NEAR + jnp.minimum(count, NEAR - 1)
        count += flags[2 * SLOTS + s]
    base[3 * SLOTS] = ZERO
    for b in range(SLOTS):
        lookup[b * 27 + 13] = b
        for d in range(26):
            slot = neighbours[b, d]
            lookup[b * 27 + d + (d > 12)] = base[jnp.where(slot < 0, 3 * SLOTS, slot - start)]


def prepare(position, neighbours, kernel_one, kernel_two):
    return pl.pallas_call(
        prepare_kernel,
        out_shape=(
            jax.ShapeDtypeStruct((2, 3, 2 * LANES, 2 * LANES), BF16),
            jax.ShapeDtypeStruct((2, 3, 2 * LANES, 2 * LANES), BF16),
            jax.ShapeDtypeStruct((27 * SLOTS,), jnp.int32),
        ),
        in_specs=[whole_smem, whole_smem, whole_vmem, whole_vmem],
        out_specs=(whole_vmem, whole_vmem, whole_smem),
        scratch_shapes=[pltpu.SMEM((32,), jnp.int32), pltpu.SMEM((32,), jnp.int32)],
        compiler_params=pltpu.CompilerParams(vmem_limit_bytes=VMEM),
        cost_estimate=pl.CostEstimate(flops=4000000, bytes_accessed=2000000, transcendentals=0),
        name="prepare",
    )(position, neighbours, kernel_one, kernel_two)


def fill_pool(own, before, after, pool, sems):
    copies = [
        pltpu.make_async_copy(own, pool.at[pl.ds(0, SLOTS)], sems.at[0]),
        pltpu.make_async_copy(before, pool.at[pl.ds(SLOTS, NEAR)], sems.at[1]),
        pltpu.make_async_copy(after, pool.at[pl.ds(SLOTS + NEAR, NEAR)], sems.at[2]),
    ]
    for copy in copies:
        copy.start()
    pool[ZERO] = jnp.zeros((VOX, LANES), BF16)
    for copy in copies:
        copy.wait()


def extend(pool, lookup, b, tile):
    def slabs(bricks, first, count):
        return [
            pool[brick, first : first + count, :].astype(F32).reshape(count // EDGE, EDGE, LANES)
            for brick in bricks
        ]

    for i in range(EDGE + 2):
        side = (i + EDGE - 1) // EDGE
        source = (i - 1) % EDGE
        bricks = [
            [lookup[b * 27 + side * 9 + j * 3 + k] for k in range(3)] for j in range(3)
        ]
        left = slabs(bricks[0], source * 64 + 48, 16)
        middle = slabs(bricks[1], source * 64, 64)
        right = slabs(bricks[2], source * 64, 16)
        low, centre, high = [
            jnp.concatenate([left[k][1:2], middle[k], right[k][0:1]], axis=0) for k in range(3)
        ]
        along = lax.broadcasted_iota(jnp.int32, centre.shape, 1)
        first = pltpu.roll(jnp.where(along == EDGE - 1, low, centre), 1, 1)
        last = pltpu.roll(jnp.where(along == 0, high, centre), EDGE - 1, 1)
        first, centre, last = [m.reshape(SLAB, LANES) for m in (first, centre, last)]
        lower = lower_half((SLAB, LANES))
        crossed = pltpu.roll(jnp.where(lower, centre, first), CH, 1)
        rows = pl.ds(i * SLAB, SLAB)
        tile[rows, 0:LANES] = jnp.where(lower, first, crossed).astype(BF16)
        tile[rows, LANES : 2 * LANES] = last.astype(BF16)
        tile[rows, 2 * LANES : 3 * LANES] = jnp.where(lower, crossed, centre).astype(BF16)


def convolve(tile, weights):
    sums = []
    for field in range(2):
        total = None
        for a in range(3):
            part = jnp.dot(
                tile[a * SLAB : a * SLAB + ROWS, field * LANES : (field + 2) * LANES],
                weights[field, a],
                preferred_element_type=F32,
            )
            total = part if total is None else total + part
        sums.append(total)

    def block(field, half):
        return sums[field][:, half * LANES : (half + 1) * LANES].reshape(
            EDGE, EDGE + 2, EDGE, LANES
        )

    zero, one = block(0, 0), block(1, 0)
    shape = (EDGE, EDGE, EDGE, LANES)
    lower = lower_half(shape)
    straight = jnp.where(lower, zero[:, 0:8], one[:, 0:8])
    crossed = jnp.where(lower, one[:, 1:9], zero[:, 1:9]).reshape(VOX, LANES)
    ends = block(0, 1)[:, 2:10] + block(1, 1)[:, 2:10]
    return (straight + ends).reshape(VOX, LANES) + pltpu.roll(crossed, CH, 1)


def row_mask(occupancy, b):
    active = occupancy[pl.ds(b, 1), :].astype(F32)
    return jnp.broadcast_to(active, (LANES, VOX)).T


def hidden_and_grad(both, mask):
    lower = lower_half((VOX, LANES))
    preact = jnp.where(lower, both, pltpu.roll(both, CH, 1))
    s = jax.nn.sigmoid(preact)
    value = jnp.where(lower, preact * s, both * s * (1.0 + preact * (1.0 - s)))
    return value * mask


def turned_over(value):
    cube = value.reshape(EDGE, EDGE, EDGE, LANES)
    turned = []
    for c in range(3):
        parts = [cube]
        if c > 0:
            parts.insert(0, jnp.zeros((EDGE, c, EDGE, LANES), F32))
        if c < 2:
            parts.append(jnp.zeros((EDGE, 2 - c, EDGE, LANES), F32))
        padded = jnp.concatenate(parts, axis=1).reshape(ROWS, LANES)
        turned.append(padded.astype(BF16).T)
    hidden = jnp.concatenate([t[:CH] for t in turned], axis=0)
    grad_pre = jnp.concatenate([t[CH:] for t in turned], axis=0)
    return hidden, grad_pre


def first_kernel(
    lookup, chosen, occupancy, weights, own, before, after,
    result, ahead, behind, terms, pool, tiles, sum_one, sum_two, sems,
):
    fill_pool(own, before, after, pool, sems)
    sum_one[...] = jnp.zeros_like(sum_one)
    sum_two[...] = jnp.zeros_like(sum_two)
    group = 4

    @pl.loop(0, SLOTS // group)
    def _(t):
        turned = []
        for p in range(group):
            extend(pool, lookup, group * t + p, tiles.at[p])
        for p in range(group):
            b = group * t + p
            value = hidden_and_grad(convolve(tiles.at[p], weights), row_mask(occupancy, b))
            result[b] = value.astype(BF16)
            turned.append(turned_over(value))
        hidden = jnp.concatenate([h for h, _ in turned], axis=1)
        grad_pre = jnp.concatenate([g for _, g in turned], axis=1)
        for a in range(3):
            def rows(first):
                return jnp.concatenate(
                    [
                        tiles[p, a * SLAB : a * SLAB + ROWS, first : first + 2 * LANES]
                        for p in range(group)
                    ],
                    axis=0,
                )

            sum_one[a] += jnp.dot(grad_pre, rows(0), preferred_element_type=F32)
            sum_two[a] += jnp.dot(hidden, rows(LANES), preferred_element_type=F32)

    for r in range(NEAR):
        ahead[r] = result[chosen[0, r]]
        behind[r] = result[chosen[1, r]]
    part = 3 * CH
    for a in range(3):
        start = a * 3 * part
        terms[start : start + part] = sum_one[a, :, 0:LANES].astype(BF16)
        terms[start + part : start + 2 * part] = sum_two[a, :, LANES:].astype(BF16)
        terms[start + 2 * part : start + 3 * part] = jnp.where(
            lower_half((part, LANES)), sum_one[a, :, LANES:], sum_two[a, :, 0:LANES]
        ).astype(BF16)
    terms[9 * part :] = jnp.zeros((TERMS - 9 * part, LANES), BF16)


def first_stage(lookup, chosen, occupancy, weights, own, before, after):
    return pl.pallas_call(
        first_kernel,
        out_shape=(
            jax.ShapeDtypeStruct((SLOTS, VOX, LANES), BF16),
            jax.ShapeDtypeStruct((NEAR, VOX, LANES), BF16),
            jax.ShapeDtypeStruct((NEAR, VOX, LANES), BF16),
            jax.ShapeDtypeStruct((TERMS, LANES), BF16),
        ),
        in_specs=[whole_smem, whole_smem, whole_vmem, whole_vmem, anywhere, anywhere, anywhere],
        out_specs=(whole_vmem,) * 4,
        scratch_shapes=[
            pltpu.VMEM((POOL, VOX, LANES), BF16),
            pltpu.VMEM((4, TILE_ROWS, 3 * LANES), BF16),
            pltpu.VMEM((3, 3 * CH, 2 * LANES), F32),
            pltpu.VMEM((3, 3 * CH, 2 * LANES), F32),
            pltpu.SemaphoreType.DMA((3,)),
        ],
        compiler_params=pltpu.CompilerParams(vmem_limit_bytes=VMEM),
        cost_estimate=pl.CostEstimate(
            flops=8000000000, bytes_accessed=6000000, transcendentals=600000
        ),
        name="first_stage",
    )(lookup, chosen, occupancy, weights, own, before, after)


def second_kernel(
    lookup, occupancy, weights, own, before, after, output, grad_in, pool, tiles, sems
):
    fill_pool(own, before, after, pool, sems)
    group = 4

    @pl.loop(0, SLOTS // group)
    def _(t):
        for p in range(group):
            extend(pool, lookup, group * t + p, tiles.at[p])
        for p in range(group):
            b = group * t + p
            both = convolve(tiles.at[p], weights).T * occupancy[pl.ds(b, 1), :].astype(F32)
            output[b] = both[:CH].astype(BF16)
            grad_in[b] = both[CH:].astype(BF16)


def second_stage(lookup, occupancy, weights, own, before, after):
    return pl.pallas_call(
        second_kernel,
        out_shape=(
            jax.ShapeDtypeStruct((SLOTS, CH, VOX), BF16),
            jax.ShapeDtypeStruct((SLOTS, CH, VOX), BF16),
        ),
        in_specs=[whole_smem, whole_vmem, whole_vmem, anywhere, anywhere, anywhere],
        out_specs=(whole_vmem,) * 2,
        scratch_shapes=[
            pltpu.VMEM((POOL, VOX, LANES), BF16),
            pltpu.VMEM((4, TILE_ROWS, 3 * LANES), BF16),
            pltpu.SemaphoreType.DMA((3,)),
        ],
        compiler_params=pltpu.CompilerParams(vmem_limit_bytes=VMEM),
        cost_estimate=pl.CostEstimate(
            flops=8000000000, bytes_accessed=6000000, transcendentals=0
        ),
        name="second_stage",
    )(lookup, occupancy, weights, own, before, after)


def combine_kernel(blocks, spread):
    count, rows = blocks.shape[0], blocks.shape[1]
    total = jnp.zeros((rows, LANES), F32)
    for d in range(count):
        total += blocks[d].astype(F32)
    spread[...] = jnp.broadcast_to(total.astype(BF16)[None], spread.shape)


def combine(blocks):
    return pl.pallas_call(
        combine_kernel,
        out_shape=jax.ShapeDtypeStruct(blocks.shape, BF16),
        in_specs=[whole_vmem],
        out_specs=whole_vmem,
        compiler_params=pltpu.CompilerParams(vmem_limit_bytes=VMEM),
        name="combine",
    )(blocks)


def unpack_kernel(scale, sums, grad_one, grad_two):
    part = 3 * CH
    for a in range(3):
        for c in range(3):
            start = a * 3 * part + c * CH
            n = 9 * a + 3 * c

            def block(which):
                return sums[start + which * part : start + which * part + CH].astype(F32) * scale

            one, two, last = block(0), block(1).T, block(2)
            grad_one[n] = one[:, :CH]
            grad_one[n + 1] = one[:, CH:]
            grad_one[n + 2] = last[:, :CH]
            grad_two[26 - n] = two[:CH]
            grad_two[25 - n] = two[CH:]
            grad_two[24 - n] = last.T[CH:]


def unpack(scale, sums):
    def kernel(*refs):
        unpack_kernel(scale, *refs)

    return pl.pallas_call(
        kernel,
        out_shape=(
            jax.ShapeDtypeStruct((27, CH, CH), F32),
            jax.ShapeDtypeStruct((27, CH, CH), F32),
        ),
        in_specs=[whole_vmem],
        out_specs=(whole_vmem,) * 2,
        compiler_params=pltpu.CompilerParams(vmem_limit_bytes=VMEM),
        name="unpack",
    )(sums)


def exchange(ahead, behind, devices):
    before = lax.ppermute(ahead, AXES, [(k, k + 1) for k in range(devices - 1)])
    after = lax.ppermute(behind, AXES, [(k + 1, k) for k in range(devices - 1)])
    return before, after


def local(devices, features, kernel_one, kernel_two, cotangent, neighbours, occupancy):
    position = lax.axis_index(AXES).astype(jnp.int32).reshape(1)
    fields, ahead, behind, chosen = pack(position, neighbours, features, cotangent, occupancy)
    before, after = exchange(ahead, behind, devices)
    first, second, lookup = prepare(position, neighbours, kernel_one, kernel_two)
    result, ahead, behind, terms = first_stage(
        lookup, chosen, occupancy, first, fields, before, after
    )
    terms = lax.all_to_all(terms, AXES, 0, 0, tiled=True)
    before, after = exchange(ahead, behind, devices)
    terms, before, after = lax.optimization_barrier((terms, before, after))
    output, grad_in = second_stage(lookup, occupancy, second, result, before, after)
    spread = combine(terms.reshape(devices, TERMS // devices, LANES)).reshape(TERMS, LANES)
    sums = lax.all_to_all(spread, AXES, 0, 0, tiled=True)
    scale = float((SLOTS * VOX * devices) ** -0.5)
    grad_one, grad_two = unpack(scale, sums)
    return output, grad_in, grad_one, grad_two


def solution(mesh):
    devices = mesh.shape["wide"] * mesh.shape["narrow"]
    bricks = P(AXES, None, None)
    in_specs = (bricks, P(), P(), bricks, P(AXES, None), P(AXES, None))
    out_specs = (bricks, bricks, P(), P())

    def run(*arrays):
        return local(devices, *arrays)

    return jax.shard_map(
        run, mesh=mesh, in_specs=in_specs, out_specs=out_specs, check_vma=False
    )
```

```python
import jax
import jax.numpy as jnp
from jax import lax
from jax.experimental import pallas as pl
from jax.experimental.pallas import tpu as pltpu
from jax.sharding import PartitionSpec as P

AXES = ("wide", "narrow")
SLOTS = 8
EDGE = 8
VOX = EDGE**3
CH = 64
LANES = 2 * CH
NEAR = 4
POOL = SLOTS + 2 * NEAR + 1
ZERO = POOL - 1
RIM = 304
SLAB = (EDGE + 2) * EDGE
TILE_ROWS = (EDGE + 2) * SLAB
ROWS = EDGE * SLAB
TERMS = 2048
HALF = TERMS // 2
VMEM = 24 * 1024 * 1024
F32 = jnp.float32
BF16 = jnp.bfloat16

whole_vmem = pl.BlockSpec(memory_space=pltpu.VMEM)
whole_smem = pl.BlockSpec(memory_space=pltpu.SMEM)
anywhere = pl.BlockSpec(memory_space=pl.ANY)


def lower_half(shape):
    return lax.broadcasted_iota(jnp.int32, shape, len(shape) - 1) < CH


def choose(position, neighbours, chosen):
    here = position[0] * SLOTS
    odd = position[0] % 2
    for r in range(SLOTS):
        chosen[0, r] = 0
        chosen[1, r] = 0
    count_ahead = jnp.int32(0)
    count_behind = jnp.int32(0)
    for b in range(SLOTS):
        highest = jnp.int32(-1)
        lowest = jnp.int32(1 << 20)
        for d in range(26):
            slot = neighbours[b, d]
            highest = jnp.maximum(highest, slot)
            lowest = jnp.minimum(lowest, jnp.where(slot < 0, 1 << 20, slot))
        chosen[odd, jnp.minimum(count_ahead, NEAR)] = b
        chosen[1 - odd, jnp.minimum(count_behind, NEAR)] = b
        count_ahead += (highest >= here + SLOTS).astype(jnp.int32)
        count_behind += (lowest < here).astype(jnp.int32)
    chosen[0, SLOTS - 1] = odd


def side_by_side(features, cotangent, occupancy, b):
    active = occupancy[pl.ds(b, 1), :].astype(F32)
    both = jnp.concatenate([features[b], cotangent[b]], axis=0).astype(F32) * active
    return both.T.astype(BF16)


def rim_rank(v):
    i, j, k = v >> 6, (v >> 3) & 7, v & 7
    inside = jnp.where(j == 0, k, jnp.where(j == 7, 20 + k, 6 + 2 * j + (k == 7).astype(jnp.int32)))
    inside = jnp.where((j == 0) | (j == 7) | (k == 0) | (k == 7), inside, RIM)
    return jnp.where(i == 0, v, jnp.where(i == 7, v - 216, 36 + 28 * i + inside))


def surface(v):
    i, j, k = v >> 6, (v >> 3) & 7, v & 7
    return (i == 0) | (i == 7) | (j == 0) | (j == 7) | (k == 0) | (k == 7)


def pack_kernel(
    position, neighbours, features_far, cotangent_far, occupancy_far,
    near_send, far_send, features, cotangent, occupancy, chosen, sems,
):
    loads = [pltpu.make_async_copy(occupancy_far, occupancy, sems.at[0])]
    for h in range(2):
        part = pl.ds(h * NEAR, NEAR)
        loads.append(
            pltpu.make_async_copy(features_far.at[part], features.at[part], sems.at[1 + h])
        )
        loads.append(
            pltpu.make_async_copy(cotangent_far.at[part], cotangent.at[part], sems.at[3 + h])
        )
    for copy in loads:
        copy.start()
    choose(position, neighbours, chosen)
    voxel = lax.broadcasted_iota(jnp.int32, (1, VOX), 1)
    rank = jnp.where(surface(voxel), rim_rank(voxel), -1)
    wanted = lax.broadcasted_iota(jnp.int32, (RIM, VOX), 0)
    select = jnp.where(rank == wanted, 1.0, 0.0).astype(BF16)
    for copy in loads:
        copy.wait()
    for side, target in ((1, far_send), (0, near_send)):
        for r in range(0, NEAR, 2):
            rows = []
            for q in range(2):
                b = chosen[side, r + q]
                active = occupancy[pl.ds(b, 1), :].astype(F32)
                rows.append((features[b].astype(F32) * active).astype(BF16))
                rows.append((cotangent[b].astype(F32) * active).astype(BF16))
            both = lax.dot_general(
                select,
                jnp.concatenate(rows, axis=0),
                (((1,), (1,)), ((), ())),
                preferred_element_type=F32,
            )
            for q in range(2):
                target[r + q] = both[:, q * LANES : (q + 1) * LANES].astype(BF16)


def pack(position, neighbours, features, cotangent, occupancy):
    return pl.pallas_call(
        pack_kernel,
        out_shape=(
            jax.ShapeDtypeStruct((NEAR, RIM, LANES), BF16),
            jax.ShapeDtypeStruct((NEAR, RIM, LANES), BF16),
        ),
        in_specs=[whole_smem, whole_smem, anywhere, anywhere, anywhere],
        out_specs=(whole_vmem, whole_vmem),
        scratch_shapes=[
            pltpu.VMEM((SLOTS, CH, VOX), BF16),
            pltpu.VMEM((SLOTS, CH, VOX), BF16),
            pltpu.VMEM((SLOTS, VOX), jnp.int32),
            pltpu.SMEM((2, SLOTS), jnp.int32),
            pltpu.SemaphoreType.DMA((5,)),
        ],
        compiler_params=pltpu.CompilerParams(vmem_limit_bytes=60 * 1024 * 1024),
        name="pack",
    )(position, neighbours, features, cotangent, occupancy)


def weight_block(kernel, flip, a, rows, columns):
    def piece(c, e):
        if c is None or e is None:
            return jnp.zeros((CH, CH), F32)
        n = 9 * a + 3 * c + e
        return kernel[26 - n if flip else n].astype(F32)

    if flip:
        block = jnp.concatenate(
            [jnp.concatenate([piece(c, e) for c in columns], axis=1) for e in rows], axis=0
        )
    else:
        block = jnp.concatenate(
            [jnp.concatenate([piece(c, e) for e in rows], axis=1) for c in columns], axis=0
        ).T
    return block.astype(BF16)


def weight_field(kernel, flip, field, target):
    rows = ((0, 1), (2, None)) if field == 0 else ((None, 2), (0, 1))
    columns = ((0, 1), (2, None)) if field == 0 else ((1, 0), (None, 2))
    for a in range(3):
        for r in range(2):
            for s in range(2):
                target[
                    field, a, r * LANES : (r + 1) * LANES, s * LANES : (s + 1) * LANES
                ] = weight_block(kernel, flip, a, rows[r], columns[s])


def prepare_kernel(
    position, neighbours, kernel_one, kernel_two, features, cotangent, occupancy,
    first, second, lookup, chosen, fields, spread, flags, base,
):
    weight_field(kernel_one, False, 0, first)
    weight_field(kernel_two, True, 1, first)
    weight_field(kernel_two, False, 0, second)
    weight_field(kernel_one, True, 1, second)
    for b in range(SLOTS):
        fields[b] = side_by_side(features, cotangent, occupancy, b)
    choose(position, neighbours, chosen)
    voxel = lax.broadcasted_iota(jnp.int32, (VOX, LANES), 0)
    rank = jnp.where(surface(voxel), rim_rank(voxel), -1)
    for first_lane in range(0, RIM, LANES):
        count = min(LANES, RIM - first_lane)
        lane = lax.broadcasted_iota(jnp.int32, (VOX, LANES), 1) + first_lane
        block = jnp.where(rank == lane, 1.0, 0.0).astype(BF16)
        spread[:, first_lane : first_lane + count] = block[:, :count]
    start = (position[0] - 1) * SLOTS
    for s in range(3 * SLOTS + 1):
        flags[s] = 0
    for b in range(SLOTS):
        for d in range(26):
            slot = neighbours[b, d]
            flags[jnp.where(slot < 0, 3 * SLOTS, slot - start)] = 1
    odd = position[0] % 2
    count = jnp.int32(0)
    for s in range(SLOTS):
        base[s] = SLOTS + NEAR * (1 - odd) + jnp.minimum(count, NEAR - 1)
        count += flags[s]
        base[SLOTS + s] = s
    count = jnp.int32(0)
    for s in range(SLOTS):
        base[2 * SLOTS + s] = SLOTS + NEAR * odd + jnp.minimum(count, NEAR - 1)
        count += flags[2 * SLOTS + s]
    base[3 * SLOTS] = ZERO
    for b in range(SLOTS):
        lookup[b * 27 + 13] = b
        for d in range(26):
            slot = neighbours[b, d]
            lookup[b * 27 + d + (d > 12)] = base[jnp.where(slot < 0, 3 * SLOTS, slot - start)]


def prepare(position, neighbours, kernel_one, kernel_two, features, cotangent, occupancy):
    return pl.pallas_call(
        prepare_kernel,
        out_shape=(
            jax.ShapeDtypeStruct((2, 3, 2 * LANES, 2 * LANES), BF16),
            jax.ShapeDtypeStruct((2, 3, 2 * LANES, 2 * LANES), BF16),
            jax.ShapeDtypeStruct((27 * SLOTS,), jnp.int32),
            jax.ShapeDtypeStruct((2, SLOTS), jnp.int32),
            jax.ShapeDtypeStruct((SLOTS, VOX, LANES), BF16),
            jax.ShapeDtypeStruct((VOX, RIM), BF16),
        ),
        in_specs=[whole_smem, whole_smem] + [whole_vmem] * 5,
        out_specs=(whole_vmem, whole_vmem, whole_smem, whole_smem) + (whole_vmem,) * 2,
        scratch_shapes=[pltpu.SMEM((32,), jnp.int32), pltpu.SMEM((32,), jnp.int32)],
        compiler_params=pltpu.CompilerParams(vmem_limit_bytes=VMEM),
        cost_estimate=pl.CostEstimate(flops=4000000, bytes_accessed=4000000, transcendentals=0),
        name="prepare",
    )(position, neighbours, kernel_one, kernel_two, features, cotangent, occupancy)


def fill_pool(own, before, after, pool, sems):
    copies = [
        pltpu.make_async_copy(own, pool.at[pl.ds(0, SLOTS)], sems.at[0]),
        pltpu.make_async_copy(before, pool.at[pl.ds(SLOTS, NEAR)], sems.at[1]),
        pltpu.make_async_copy(after, pool.at[pl.ds(SLOTS + NEAR, NEAR)], sems.at[2]),
    ]
    for copy in copies:
        copy.start()
    pool[ZERO] = jnp.zeros((VOX, LANES), BF16)
    for copy in copies:
        copy.wait()


def extend(pool, lookup, b, tile):
    def slabs(bricks, first, count):
        return [
            pool[brick, first : first + count, :].astype(F32).reshape(count // EDGE, EDGE, LANES)
            for brick in bricks
        ]

    for i in range(EDGE + 2):
        side = (i + EDGE - 1) // EDGE
        source = (i - 1) % EDGE
        bricks = [
            [lookup[b * 27 + side * 9 + j * 3 + k] for k in range(3)] for j in range(3)
        ]
        left = slabs(bricks[0], source * 64 + 48, 16)
        middle = slabs(bricks[1], source * 64, 64)
        right = slabs(bricks[2], source * 64, 16)
        low, centre, high = [
            jnp.concatenate([left[k][1:2], middle[k], right[k][0:1]], axis=0) for k in range(3)
        ]
        along = lax.broadcasted_iota(jnp.int32, centre.shape, 1)
        first = pltpu.roll(jnp.where(along == EDGE - 1, low, centre), 1, 1)
        last = pltpu.roll(jnp.where(along == 0, high, centre), EDGE - 1, 1)
        first, centre, last = [m.reshape(SLAB, LANES) for m in (first, centre, last)]
        lower = lower_half((SLAB, LANES))
        crossed = pltpu.roll(jnp.where(lower, centre, first), CH, 1)
        rows = pl.ds(i * SLAB, SLAB)
        tile[rows, 0:LANES] = jnp.where(lower, first, crossed).astype(BF16)
        tile[rows, LANES : 2 * LANES] = last.astype(BF16)
        tile[rows, 2 * LANES : 3 * LANES] = jnp.where(lower, crossed, centre).astype(BF16)


def convolve(tile, weights):
    sums = []
    for field in range(2):
        total = None
        for a in range(3):
            part = jnp.dot(
                tile[a * SLAB : a * SLAB + ROWS, field * LANES : (field + 2) * LANES],
                weights[field, a],
                preferred_element_type=F32,
            )
            total = part if total is None else total + part
        sums.append(total)

    def block(field, half):
        return sums[field][:, half * LANES : (half + 1) * LANES].reshape(
            EDGE, EDGE + 2, EDGE, LANES
        )

    zero, one = block(0, 0), block(1, 0)
    shape = (EDGE, EDGE, EDGE, LANES)
    lower = lower_half(shape)
    straight = jnp.where(lower, zero[:, 0:8], one[:, 0:8])
    crossed = jnp.where(lower, one[:, 1:9], zero[:, 1:9]).reshape(VOX, LANES)
    ends = block(0, 1)[:, 2:10] + block(1, 1)[:, 2:10]
    return (straight + ends).reshape(VOX, LANES) + pltpu.roll(crossed, CH, 1)


def row_mask(occupancy, b):
    active = occupancy[pl.ds(b, 1), :].astype(F32)
    return jnp.broadcast_to(active, (LANES, VOX)).T


def hidden_and_grad(both, mask):
    lower = lower_half((VOX, LANES))
    preact = jnp.where(lower, both, pltpu.roll(both, CH, 1))
    s = jax.nn.sigmoid(preact)
    value = jnp.where(lower, preact * s, both * s * (1.0 + preact * (1.0 - s)))
    return value * mask


def turned_over(value):
    cube = value.reshape(EDGE, EDGE, EDGE, LANES)
    turned = []
    for c in range(3):
        parts = [cube]
        if c > 0:
            parts.insert(0, jnp.zeros((EDGE, c, EDGE, LANES), F32))
        if c < 2:
            parts.append(jnp.zeros((EDGE, 2 - c, EDGE, LANES), F32))
        padded = jnp.concatenate(parts, axis=1).reshape(ROWS, LANES)
        turned.append(padded.astype(BF16).T)
    hidden = jnp.concatenate([t[:CH] for t in turned], axis=0)
    grad_pre = jnp.concatenate([t[CH:] for t in turned], axis=0)
    return hidden, grad_pre


def first_kernel(
    lookup, chosen, occupancy, weights, spread, near, far, own,
    result, ahead, behind, given, kept, pool, tiles, sum_one, sum_two, terms, sems,
):
    load = pltpu.make_async_copy(own, pool.at[pl.ds(0, SLOTS)], sems.at[0])
    load.start()
    pool[ZERO] = jnp.zeros((VOX, LANES), BF16)
    for place, rim in ((SLOTS, near), (SLOTS + NEAR, far)):
        for r in range(0, NEAR, 2):
            whole = jnp.dot(
                spread[...],
                jnp.concatenate([rim[r], rim[r + 1]], axis=1),
                preferred_element_type=F32,
            )
            for q in range(2):
                pool[place + r + q] = whole[:, q * LANES : (q + 1) * LANES].astype(BF16)
    load.wait()
    sum_one[...] = jnp.zeros_like(sum_one)
    sum_two[...] = jnp.zeros_like(sum_two)
    group = 4

    @pl.loop(0, SLOTS // group)
    def _(t):
        turned = []
        for p in range(group):
            extend(pool, lookup, group * t + p, tiles.at[p])
        for p in range(group):
            b = group * t + p
            value = hidden_and_grad(convolve(tiles.at[p], weights), row_mask(occupancy, b))
            result[b] = value.astype(BF16)
            turned.append(turned_over(value))
        hidden = jnp.concatenate([h for h, _ in turned], axis=1)
        grad_pre = jnp.concatenate([g for _, g in turned], axis=1)
        for a in range(3):
            def rows(first):
                return jnp.concatenate(
                    [
                        tiles[p, a * SLAB : a * SLAB + ROWS, first : first + 2 * LANES]
                        for p in range(group)
                    ],
                    axis=0,
                )

            sum_one[a] += jnp.dot(grad_pre, rows(0), preferred_element_type=F32)
            sum_two[a] += jnp.dot(hidden, rows(LANES), preferred_element_type=F32)

    for r in range(NEAR):
        ahead[r] = result[chosen[0, r]]
        behind[r] = result[chosen[1, r]]
    part = 3 * CH
    for a in range(3):
        start = a * 3 * part
        terms[start : start + part] = sum_one[a, :, 0:LANES]
        terms[start + part : start + 2 * part] = sum_two[a, :, LANES:]
        terms[start + 2 * part : start + 3 * part] = jnp.where(
            lower_half((part, LANES)), sum_one[a, :, LANES:], sum_two[a, :, 0:LANES]
        )
    terms[9 * part :] = jnp.zeros((TERMS - 9 * part, LANES), F32)
    odd = chosen[0, SLOTS - 1]
    given[...] = terms[pl.ds(pl.multiple_of((1 - odd) * HALF, HALF), HALF), :].astype(BF16)
    kept[...] = terms[pl.ds(pl.multiple_of(odd * HALF, HALF), HALF), :]


def first_stage(lookup, chosen, occupancy, weights, spread, near, far, own):
    return pl.pallas_call(
        first_kernel,
        out_shape=(
            jax.ShapeDtypeStruct((SLOTS, VOX, LANES), BF16),
            jax.ShapeDtypeStruct((NEAR, VOX, LANES), BF16),
            jax.ShapeDtypeStruct((NEAR, VOX, LANES), BF16),
            jax.ShapeDtypeStruct((HALF, LANES), BF16),
            jax.ShapeDtypeStruct((HALF, LANES), F32),
        ),
        in_specs=[whole_smem, whole_smem] + [whole_vmem] * 5 + [anywhere],
        out_specs=(whole_vmem,) * 5,
        scratch_shapes=[
            pltpu.VMEM((POOL, VOX, LANES), BF16),
            pltpu.VMEM((4, TILE_ROWS, 3 * LANES), BF16),
            pltpu.VMEM((3, 3 * CH, 2 * LANES), F32),
            pltpu.VMEM((3, 3 * CH, 2 * LANES), F32),
            pltpu.VMEM((TERMS, LANES), F32),
            pltpu.SemaphoreType.DMA((3,)),
        ],
        compiler_params=pltpu.CompilerParams(vmem_limit_bytes=VMEM),
        cost_estimate=pl.CostEstimate(
            flops=8000000000, bytes_accessed=6000000, transcendentals=600000
        ),
        name="first_stage",
    )(lookup, chosen, occupancy, weights, spread, near, far, own)


def second_kernel(
    lookup, occupancy, weights, own, before, after, output, grad_in, pool, tiles, sems
):
    fill_pool(own, before, after, pool, sems)
    group = 4

    @pl.loop(0, SLOTS // group)
    def _(t):
        for p in range(group):
            extend(pool, lookup, group * t + p, tiles.at[p])
        for p in range(group):
            b = group * t + p
            both = convolve(tiles.at[p], weights).T * occupancy[pl.ds(b, 1), :].astype(F32)
            output[b] = both[:CH].astype(BF16)
            grad_in[b] = both[CH:].astype(BF16)


def second_stage(lookup, occupancy, weights, own, before, after):
    return pl.pallas_call(
        second_kernel,
        out_shape=(
            jax.ShapeDtypeStruct((SLOTS, CH, VOX), BF16),
            jax.ShapeDtypeStruct((SLOTS, CH, VOX), BF16),
        ),
        in_specs=[whole_smem, whole_vmem, whole_vmem, anywhere, anywhere, anywhere],
        out_specs=(whole_vmem,) * 2,
        scratch_shapes=[
            pltpu.VMEM((POOL, VOX, LANES), BF16),
            pltpu.VMEM((4, TILE_ROWS, 3 * LANES), BF16),
            pltpu.SemaphoreType.DMA((3,)),
        ],
        compiler_params=pltpu.CompilerParams(vmem_limit_bytes=VMEM),
        cost_estimate=pl.CostEstimate(
            flops=8000000000, bytes_accessed=6000000, transcendentals=0
        ),
        name="second_stage",
    )(lookup, occupancy, weights, own, before, after)


def pair_kernel(kept, received, total):
    total[...] = (kept[...] + received[...].astype(F32)).astype(BF16)


def pair_sum(kept, received):
    return pl.pallas_call(
        pair_kernel,
        out_shape=jax.ShapeDtypeStruct((HALF, LANES), BF16),
        in_specs=[whole_vmem] * 2,
        out_specs=whole_vmem,
        compiler_params=pltpu.CompilerParams(vmem_limit_bytes=VMEM),
        name="pair_sum",
    )(kept, received)


def combine_kernel(blocks, spread):
    count, rows = blocks.shape[0], blocks.shape[1]
    total = jnp.zeros((rows, LANES), F32)
    for d in range(count):
        total += blocks[d].astype(F32)
    spread[...] = jnp.broadcast_to(total.astype(BF16)[None], spread.shape)


def combine(blocks):
    return pl.pallas_call(
        combine_kernel,
        out_shape=jax.ShapeDtypeStruct(blocks.shape, BF16),
        in_specs=[whole_vmem],
        out_specs=whole_vmem,
        compiler_params=pltpu.CompilerParams(vmem_limit_bytes=VMEM),
        name="combine",
    )(blocks)


def unpack_kernel(scale, position, own, other, grad_one, grad_two, sums):
    odd = position[0] % 2
    sums[pl.ds(pl.multiple_of(odd * HALF, HALF), HALF), :] = own[...]
    sums[pl.ds(pl.multiple_of((1 - odd) * HALF, HALF), HALF), :] = other[...]
    part = 3 * CH
    for a in range(3):
        for c in range(3):
            start = a * 3 * part + c * CH
            n = 9 * a + 3 * c

            def block(which):
                return sums[start + which * part : start + which * part + CH].astype(F32) * scale

            one, two, last = block(0), block(1).T, block(2)
            grad_one[n] = one[:, :CH]
            grad_one[n + 1] = one[:, CH:]
            grad_one[n + 2] = last[:, :CH]
            grad_two[26 - n] = two[:CH]
            grad_two[25 - n] = two[CH:]
            grad_two[24 - n] = last.T[CH:]


def unpack(scale, position, own, other):
    def kernel(*refs):
        unpack_kernel(scale, *refs)

    return pl.pallas_call(
        kernel,
        out_shape=(
            jax.ShapeDtypeStruct((27, CH, CH), F32),
            jax.ShapeDtypeStruct((27, CH, CH), F32),
        ),
        in_specs=[whole_smem, whole_vmem, whole_vmem],
        out_specs=(whole_vmem,) * 2,
        scratch_shapes=[pltpu.VMEM((TERMS, LANES), BF16)],
        compiler_params=pltpu.CompilerParams(vmem_limit_bytes=VMEM),
        name="unpack",
    )(position, own, other)


def near_swap(rows, devices):
    return lax.ppermute(rows, AXES, [(k, k ^ 1) for k in range(devices)])


def far_swap(rows, devices):
    route = [(k, k + 1) for k in range(1, devices - 1, 2)]
    route += [(k + 1, k) for k in range(1, devices - 1, 2)]
    return lax.ppermute(rows, AXES, route)


def local(devices, features, kernel_one, kernel_two, cotangent, neighbours, occupancy):
    position = lax.axis_index(AXES).astype(jnp.int32).reshape(1)
    near_send, far_send = pack(position, neighbours, features, cotangent, occupancy)
    near_send, far_send, later = lax.optimization_barrier((near_send, far_send, position))
    far = far_swap(far_send, devices)
    near = near_swap(near_send, devices)
    first, second, lookup, chosen, fields, spread = prepare(
        later, neighbours, kernel_one, kernel_two, features, cotangent, occupancy
    )
    result, near_send, far_send, given, kept = first_stage(
        lookup, chosen, occupancy, first, spread, near, far, fields
    )
    cores = [list(range(c, devices, 2)) for c in range(2)]
    blocks = devices // 2

    def to_all(rows):
        return lax.all_to_all(rows, AXES, 0, 0, axis_index_groups=cores, tiled=True)

    terms = to_all(pair_sum(kept, near_swap(given, devices)))
    far = far_swap(far_send, devices)
    near = near_swap(near_send, devices)
    terms, near, far = lax.optimization_barrier((terms, near, far))
    output, grad_in = second_stage(lookup, occupancy, second, result, near, far)
    spread = combine(terms.reshape(blocks, HALF // blocks, LANES)).reshape(HALF, LANES)
    own = to_all(spread)
    own, output, grad_in = lax.optimization_barrier((own, output, grad_in))
    other = near_swap(own, devices)
    scale = float((SLOTS * VOX * devices) ** -0.5)
    grad_one, grad_two = unpack(scale, position, own, other)
    return output, grad_in, grad_one, grad_two


def solution(mesh):
    devices = mesh.shape["wide"] * mesh.shape["narrow"]
    bricks = P(AXES, None, None)
    in_specs = (bricks, P(), P(), bricks, P(AXES, None), P(AXES, None))
    out_specs = (bricks, bricks, P(), P())

    def run(*arrays):
        return local(devices, *arrays)

    return jax.shard_map(
        run, mesh=mesh, in_specs=in_specs, out_specs=out_specs, check_vma=False
    )
```

```python
import jax
import jax.numpy as jnp
from jax import lax
from jax.experimental import pallas as pl
from jax.experimental.pallas import tpu as pltpu
from jax.sharding import PartitionSpec as P

AXES = ("wide", "narrow")
SLOTS = 8
EDGE = 8
VOX = EDGE**3
CH = 64
LANES = 2 * CH
NEAR = 4
POOL = SLOTS + 2 * NEAR + 1
ZERO = POOL - 1
RIM = 304
SLAB = (EDGE + 2) * EDGE
TILE_ROWS = (EDGE + 2) * SLAB
ROWS = EDGE * SLAB
TERMS = 2048
HALF = TERMS // 2
VMEM = 24 * 1024 * 1024
F32 = jnp.float32
BF16 = jnp.bfloat16

whole_vmem = pl.BlockSpec(memory_space=pltpu.VMEM)
whole_smem = pl.BlockSpec(memory_space=pltpu.SMEM)
anywhere = pl.BlockSpec(memory_space=pl.ANY)


def lower_half(shape):
    return lax.broadcasted_iota(jnp.int32, shape, len(shape) - 1) < CH


def choose(position, neighbours, chosen):
    here = position[0] * SLOTS
    odd = position[0] % 2
    for r in range(SLOTS):
        chosen[0, r] = 0
        chosen[1, r] = 0
    count_ahead = jnp.int32(0)
    count_behind = jnp.int32(0)
    for b in range(SLOTS):
        highest = jnp.int32(-1)
        lowest = jnp.int32(1 << 20)
        for d in range(26):
            slot = neighbours[b, d]
            highest = jnp.maximum(highest, slot)
            lowest = jnp.minimum(lowest, jnp.where(slot < 0, 1 << 20, slot))
        chosen[odd, jnp.minimum(count_ahead, NEAR)] = b
        chosen[1 - odd, jnp.minimum(count_behind, NEAR)] = b
        count_ahead += (highest >= here + SLOTS).astype(jnp.int32)
        count_behind += (lowest < here).astype(jnp.int32)
    chosen[0, SLOTS - 1] = odd


def side_by_side(features, cotangent, occupancy, b):
    active = occupancy[pl.ds(b, 1), :].astype(F32)
    both = jnp.concatenate([features[b], cotangent[b]], axis=0).astype(F32) * active
    return both.T.astype(BF16)


def rim_rank(v):
    i, j, k = v >> 6, (v >> 3) & 7, v & 7
    inside = jnp.where(j == 0, k, jnp.where(j == 7, 20 + k, 6 + 2 * j + (k == 7).astype(jnp.int32)))
    inside = jnp.where((j == 0) | (j == 7) | (k == 0) | (k == 7), inside, RIM)
    return jnp.where(i == 0, v, jnp.where(i == 7, v - 216, 36 + 28 * i + inside))


def surface(v):
    i, j, k = v >> 6, (v >> 3) & 7, v & 7
    return (i == 0) | (i == 7) | (j == 0) | (j == 7) | (k == 0) | (k == 7)


def pack_kernel(
    position, neighbours, features_far, cotangent_far, occupancy_far,
    near_send, far_send, features, cotangent, occupancy, chosen, sems,
):
    loads = [pltpu.make_async_copy(occupancy_far, occupancy, sems.at[0])]
    for h in range(2):
        part = pl.ds(h * NEAR, NEAR)
        loads.append(
            pltpu.make_async_copy(features_far.at[part], features.at[part], sems.at[1 + h])
        )
        loads.append(
            pltpu.make_async_copy(cotangent_far.at[part], cotangent.at[part], sems.at[3 + h])
        )
    for copy in loads:
        copy.start()
    choose(position, neighbours, chosen)
    voxel = lax.broadcasted_iota(jnp.int32, (1, VOX), 1)
    rank = jnp.where(surface(voxel), rim_rank(voxel), -1)
    wanted = lax.broadcasted_iota(jnp.int32, (RIM, VOX), 0)
    select = jnp.where(rank == wanted, 1.0, 0.0).astype(BF16)
    for copy in loads:
        copy.wait()
    for side, target in ((1, far_send), (0, near_send)):
        for r in range(0, NEAR, 2):
            rows = []
            for q in range(2):
                b = chosen[side, r + q]
                active = occupancy[pl.ds(b, 1), :].astype(F32)
                rows.append((features[b].astype(F32) * active).astype(BF16))
                rows.append((cotangent[b].astype(F32) * active).astype(BF16))
            both = lax.dot_general(
                select,
                jnp.concatenate(rows, axis=0),
                (((1,), (1,)), ((), ())),
                preferred_element_type=F32,
            )
            for q in range(2):
                target[r + q] = both[:, q * LANES : (q + 1) * LANES].astype(BF16)


def pack(position, neighbours, features, cotangent, occupancy):
    return pl.pallas_call(
        pack_kernel,
        out_shape=(
            jax.ShapeDtypeStruct((NEAR, RIM, LANES), BF16),
            jax.ShapeDtypeStruct((NEAR, RIM, LANES), BF16),
        ),
        in_specs=[whole_smem, whole_smem, anywhere, anywhere, anywhere],
        out_specs=(whole_vmem, whole_vmem),
        scratch_shapes=[
            pltpu.VMEM((SLOTS, CH, VOX), BF16),
            pltpu.VMEM((SLOTS, CH, VOX), BF16),
            pltpu.VMEM((SLOTS, VOX), jnp.int32),
            pltpu.SMEM((2, SLOTS), jnp.int32),
            pltpu.SemaphoreType.DMA((5,)),
        ],
        compiler_params=pltpu.CompilerParams(vmem_limit_bytes=60 * 1024 * 1024),
        name="pack",
    )(position, neighbours, features, cotangent, occupancy)


def weight_block(kernel, flip, a, rows, columns):
    def piece(c, e):
        if c is None or e is None:
            return jnp.zeros((CH, CH), F32)
        n = 9 * a + 3 * c + e
        return kernel[26 - n if flip else n].astype(F32)

    if flip:
        block = jnp.concatenate(
            [jnp.concatenate([piece(c, e) for c in columns], axis=1) for e in rows], axis=0
        )
    else:
        block = jnp.concatenate(
            [jnp.concatenate([piece(c, e) for e in rows], axis=1) for c in columns], axis=0
        ).T
    return block.astype(BF16)


def weight_field(kernel, flip, field, target):
    rows = ((0, 1), (2, None)) if field == 0 else ((None, 2), (0, 1))
    columns = ((0, 1), (2, None)) if field == 0 else ((1, 0), (None, 2))
    for a in range(3):
        for r in range(2):
            for s in range(2):
                target[
                    field, a, r * LANES : (r + 1) * LANES, s * LANES : (s + 1) * LANES
                ] = weight_block(kernel, flip, a, rows[r], columns[s])


def prepare_kernel(
    position, neighbours, kernel_one, kernel_two, features, cotangent, occupancy,
    first, lookup, chosen, fields, spread, flags, base,
):
    weight_field(kernel_one, False, 0, first)
    weight_field(kernel_two, True, 1, first)
    for b in range(SLOTS):
        fields[b] = side_by_side(features, cotangent, occupancy, b)
    choose(position, neighbours, chosen)
    voxel = lax.broadcasted_iota(jnp.int32, (VOX, LANES), 0)
    rank = jnp.where(surface(voxel), rim_rank(voxel), -1)
    for first_lane in range(0, RIM, LANES):
        count = min(LANES, RIM - first_lane)
        lane = lax.broadcasted_iota(jnp.int32, (VOX, LANES), 1) + first_lane
        block = jnp.where(rank == lane, 1.0, 0.0).astype(BF16)
        spread[:, first_lane : first_lane + count] = block[:, :count]
    start = (position[0] - 1) * SLOTS
    for s in range(3 * SLOTS + 1):
        flags[s] = 0
    for b in range(SLOTS):
        for d in range(26):
            slot = neighbours[b, d]
            flags[jnp.where(slot < 0, 3 * SLOTS, slot - start)] = 1
    odd = position[0] % 2
    count = jnp.int32(0)
    for s in range(SLOTS):
        base[s] = SLOTS + NEAR * (1 - odd) + jnp.minimum(count, NEAR - 1)
        count += flags[s]
        base[SLOTS + s] = s
    count = jnp.int32(0)
    for s in range(SLOTS):
        base[2 * SLOTS + s] = SLOTS + NEAR * odd + jnp.minimum(count, NEAR - 1)
        count += flags[2 * SLOTS + s]
    base[3 * SLOTS] = ZERO
    for b in range(SLOTS):
        lookup[b * 27 + 13] = b
        for d in range(26):
            slot = neighbours[b, d]
            lookup[b * 27 + d + (d > 12)] = base[jnp.where(slot < 0, 3 * SLOTS, slot - start)]


def prepare(position, neighbours, kernel_one, kernel_two, features, cotangent, occupancy):
    return pl.pallas_call(
        prepare_kernel,
        out_shape=(
            jax.ShapeDtypeStruct((2, 3, 2 * LANES, 2 * LANES), BF16),
            jax.ShapeDtypeStruct((27 * SLOTS,), jnp.int32),
            jax.ShapeDtypeStruct((2, SLOTS), jnp.int32),
            jax.ShapeDtypeStruct((SLOTS, VOX, LANES), BF16),
            jax.ShapeDtypeStruct((VOX, RIM), BF16),
        ),
        in_specs=[whole_smem, whole_smem] + [whole_vmem] * 5,
        out_specs=(whole_vmem, whole_smem, whole_smem) + (whole_vmem,) * 2,
        scratch_shapes=[pltpu.SMEM((32,), jnp.int32), pltpu.SMEM((32,), jnp.int32)],
        compiler_params=pltpu.CompilerParams(vmem_limit_bytes=VMEM),
        cost_estimate=pl.CostEstimate(flops=4000000, bytes_accessed=4000000, transcendentals=0),
        name="prepare",
    )(position, neighbours, kernel_one, kernel_two, features, cotangent, occupancy)


def relay_kernel(
    after, chosen, kernel_one, kernel_two, result, second, near_send, far_send
):
    for r in range(NEAR):
        far_send[r] = result[chosen[1, r]]
        near_send[r] = result[chosen[0, r]]
    weight_field(kernel_two, False, 0, second)
    weight_field(kernel_one, True, 1, second)


def relay(after, chosen, kernel_one, kernel_two, result):
    return pl.pallas_call(
        relay_kernel,
        out_shape=(
            jax.ShapeDtypeStruct((2, 3, 2 * LANES, 2 * LANES), BF16),
            jax.ShapeDtypeStruct((NEAR, VOX, LANES), BF16),
            jax.ShapeDtypeStruct((NEAR, VOX, LANES), BF16),
        ),
        in_specs=[whole_smem, whole_smem] + [whole_vmem] * 3,
        out_specs=(whole_vmem,) * 3,
        compiler_params=pltpu.CompilerParams(vmem_limit_bytes=VMEM),
        cost_estimate=pl.CostEstimate(
            flops=5000000000, bytes_accessed=2000000, transcendentals=0
        ),
        name="relay",
    )(after, chosen, kernel_one, kernel_two, result)


def fill_pool(own, before, after, pool, sems):
    copies = [
        pltpu.make_async_copy(own, pool.at[pl.ds(0, SLOTS)], sems.at[0]),
        pltpu.make_async_copy(before, pool.at[pl.ds(SLOTS, NEAR)], sems.at[1]),
        pltpu.make_async_copy(after, pool.at[pl.ds(SLOTS + NEAR, NEAR)], sems.at[2]),
    ]
    for copy in copies:
        copy.start()
    pool[ZERO] = jnp.zeros((VOX, LANES), BF16)
    for copy in copies:
        copy.wait()


def extend(pool, lookup, b, tile):
    def slabs(bricks, first, count):
        return [
            pool[brick, first : first + count, :].astype(F32).reshape(count // EDGE, EDGE, LANES)
            for brick in bricks
        ]

    for i in range(EDGE + 2):
        side = (i + EDGE - 1) // EDGE
        source = (i - 1) % EDGE
        bricks = [
            [lookup[b * 27 + side * 9 + j * 3 + k] for k in range(3)] for j in range(3)
        ]
        left = slabs(bricks[0], source * 64 + 48, 16)
        middle = slabs(bricks[1], source * 64, 64)
        right = slabs(bricks[2], source * 64, 16)
        low, centre, high = [
            jnp.concatenate([left[k][1:2], middle[k], right[k][0:1]], axis=0) for k in range(3)
        ]
        along = lax.broadcasted_iota(jnp.int32, centre.shape, 1)
        first = pltpu.roll(jnp.where(along == EDGE - 1, low, centre), 1, 1)
        last = pltpu.roll(jnp.where(along == 0, high, centre), EDGE - 1, 1)
        first, centre, last = [m.reshape(SLAB, LANES) for m in (first, centre, last)]
        lower = lower_half((SLAB, LANES))
        crossed = pltpu.roll(jnp.where(lower, centre, first), CH, 1)
        rows = pl.ds(i * SLAB, SLAB)
        tile[rows, 0:LANES] = jnp.where(lower, first, crossed).astype(BF16)
        tile[rows, LANES : 2 * LANES] = last.astype(BF16)
        tile[rows, 2 * LANES : 3 * LANES] = jnp.where(lower, crossed, centre).astype(BF16)


def convolve(tile, weights):
    sums = []
    for field in range(2):
        total = None
        for a in range(3):
            part = jnp.dot(
                tile[a * SLAB : a * SLAB + ROWS, field * LANES : (field + 2) * LANES],
                weights[field, a],
                preferred_element_type=F32,
            )
            total = part if total is None else total + part
        sums.append(total)

    def block(field, half):
        return sums[field][:, half * LANES : (half + 1) * LANES].reshape(
            EDGE, EDGE + 2, EDGE, LANES
        )

    zero, one = block(0, 0), block(1, 0)
    shape = (EDGE, EDGE, EDGE, LANES)
    lower = lower_half(shape)
    straight = jnp.where(lower, zero[:, 0:8], one[:, 0:8])
    crossed = jnp.where(lower, one[:, 1:9], zero[:, 1:9]).reshape(VOX, LANES)
    ends = block(0, 1)[:, 2:10] + block(1, 1)[:, 2:10]
    return (straight + ends).reshape(VOX, LANES) + pltpu.roll(crossed, CH, 1)


def row_mask(occupancy, b):
    active = occupancy[pl.ds(b, 1), :].astype(F32)
    return jnp.broadcast_to(active, (LANES, VOX)).T


def hidden_and_grad(both, mask):
    lower = lower_half((VOX, LANES))
    preact = jnp.where(lower, both, pltpu.roll(both, CH, 1))
    s = jax.nn.sigmoid(preact)
    value = jnp.where(lower, preact * s, both * s * (1.0 + preact * (1.0 - s)))
    return value * mask


def turned_over(value):
    cube = value.reshape(EDGE, EDGE, EDGE, LANES)
    turned = []
    for c in range(3):
        parts = [cube]
        if c > 0:
            parts.insert(0, jnp.zeros((EDGE, c, EDGE, LANES), F32))
        if c < 2:
            parts.append(jnp.zeros((EDGE, 2 - c, EDGE, LANES), F32))
        padded = jnp.concatenate(parts, axis=1).reshape(ROWS, LANES)
        turned.append(padded.astype(BF16).T)
    hidden = jnp.concatenate([t[:CH] for t in turned], axis=0)
    grad_pre = jnp.concatenate([t[CH:] for t in turned], axis=0)
    return hidden, grad_pre


def first_kernel(
    lookup, chosen, occupancy, weights, spread, near, far, own,
    result, given, kept, pool, tiles, sum_one, sum_two, terms, sems,
):
    load = pltpu.make_async_copy(own, pool.at[pl.ds(0, SLOTS)], sems.at[0])
    load.start()
    pool[ZERO] = jnp.zeros((VOX, LANES), BF16)
    for place, rim in ((SLOTS, near), (SLOTS + NEAR, far)):
        for r in range(0, NEAR, 2):
            whole = jnp.dot(
                spread[...],
                jnp.concatenate([rim[r], rim[r + 1]], axis=1),
                preferred_element_type=F32,
            )
            for q in range(2):
                pool[place + r + q] = whole[:, q * LANES : (q + 1) * LANES].astype(BF16)
    load.wait()
    sum_one[...] = jnp.zeros_like(sum_one)
    sum_two[...] = jnp.zeros_like(sum_two)
    group = 4

    @pl.loop(0, SLOTS // group)
    def _(t):
        turned = []
        for p in range(group):
            extend(pool, lookup, group * t + p, tiles.at[p])
        for p in range(group):
            b = group * t + p
            value = hidden_and_grad(convolve(tiles.at[p], weights), row_mask(occupancy, b))
            result[b] = value.astype(BF16)
            turned.append(turned_over(value))
        hidden = jnp.concatenate([h for h, _ in turned], axis=1)
        grad_pre = jnp.concatenate([g for _, g in turned], axis=1)
        for a in range(3):
            def rows(first):
                return jnp.concatenate(
                    [
                        tiles[p, a * SLAB : a * SLAB + ROWS, first : first + 2 * LANES]
                        for p in range(group)
                    ],
                    axis=0,
                )

            sum_one[a] += jnp.dot(grad_pre, rows(0), preferred_element_type=F32)
            sum_two[a] += jnp.dot(hidden, rows(LANES), preferred_element_type=F32)

    part = 3 * CH
    for a in range(3):
        start = a * 3 * part
        terms[start : start + part] = sum_one[a, :, 0:LANES]
        terms[start + part : start + 2 * part] = sum_two[a, :, LANES:]
        terms[start + 2 * part : start + 3 * part] = jnp.where(
            lower_half((part, LANES)), sum_one[a, :, LANES:], sum_two[a, :, 0:LANES]
        )
    terms[9 * part :] = jnp.zeros((TERMS - 9 * part, LANES), F32)
    odd = chosen[0, SLOTS - 1]
    given[...] = terms[pl.ds(pl.multiple_of((1 - odd) * HALF, HALF), HALF), :].astype(BF16)
    kept[...] = terms[pl.ds(pl.multiple_of(odd * HALF, HALF), HALF), :]


def first_stage(lookup, chosen, occupancy, weights, spread, near, far, own):
    return pl.pallas_call(
        first_kernel,
        out_shape=(
            jax.ShapeDtypeStruct((SLOTS, VOX, LANES), BF16),
            jax.ShapeDtypeStruct((HALF, LANES), BF16),
            jax.ShapeDtypeStruct((HALF, LANES), F32),
        ),
        in_specs=[whole_smem, whole_smem] + [whole_vmem] * 5 + [anywhere],
        out_specs=(whole_vmem,) * 3,
        scratch_shapes=[
            pltpu.VMEM((POOL, VOX, LANES), BF16),
            pltpu.VMEM((4, TILE_ROWS, 3 * LANES), BF16),
            pltpu.VMEM((3, 3 * CH, 2 * LANES), F32),
            pltpu.VMEM((3, 3 * CH, 2 * LANES), F32),
            pltpu.VMEM((TERMS, LANES), F32),
            pltpu.SemaphoreType.DMA((3,)),
        ],
        compiler_params=pltpu.CompilerParams(vmem_limit_bytes=VMEM),
        cost_estimate=pl.CostEstimate(
            flops=8000000000, bytes_accessed=6000000, transcendentals=600000
        ),
        name="first_stage",
    )(lookup, chosen, occupancy, weights, spread, near, far, own)


def second_kernel(
    lookup, occupancy, weights, own, before, after, output, grad_in, pool, tiles, sems
):
    fill_pool(own, before, after, pool, sems)
    group = 4

    @pl.loop(0, SLOTS // group)
    def _(t):
        for p in range(group):
            extend(pool, lookup, group * t + p, tiles.at[p])
        for p in range(group):
            b = group * t + p
            both = convolve(tiles.at[p], weights).T * occupancy[pl.ds(b, 1), :].astype(F32)
            output[b] = both[:CH].astype(BF16)
            grad_in[b] = both[CH:].astype(BF16)


def second_stage(lookup, occupancy, weights, own, before, after):
    return pl.pallas_call(
        second_kernel,
        out_shape=(
            jax.ShapeDtypeStruct((SLOTS, CH, VOX), BF16),
            jax.ShapeDtypeStruct((SLOTS, CH, VOX), BF16),
        ),
        in_specs=[whole_smem, whole_vmem, whole_vmem, anywhere, anywhere, anywhere],
        out_specs=(whole_vmem,) * 2,
        scratch_shapes=[
            pltpu.VMEM((POOL, VOX, LANES), BF16),
            pltpu.VMEM((4, TILE_ROWS, 3 * LANES), BF16),
            pltpu.SemaphoreType.DMA((3,)),
        ],
        compiler_params=pltpu.CompilerParams(vmem_limit_bytes=VMEM),
        cost_estimate=pl.CostEstimate(
            flops=8000000000, bytes_accessed=6000000, transcendentals=0
        ),
        name="second_stage",
    )(lookup, occupancy, weights, own, before, after)


def pair_kernel(kept, received, total):
    total[...] = (kept[...] + received[...].astype(F32)).astype(BF16)


def pair_sum(kept, received):
    return pl.pallas_call(
        pair_kernel,
        out_shape=jax.ShapeDtypeStruct((HALF, LANES), BF16),
        in_specs=[whole_vmem] * 2,
        out_specs=whole_vmem,
        compiler_params=pltpu.CompilerParams(vmem_limit_bytes=VMEM),
        name="pair_sum",
    )(kept, received)


def combine_kernel(blocks, spread):
    count, rows = blocks.shape[0], blocks.shape[1]
    total = jnp.zeros((rows, LANES), F32)
    for d in range(count):
        total += blocks[d].astype(F32)
    spread[...] = jnp.broadcast_to(total.astype(BF16)[None], spread.shape)


def combine(blocks):
    return pl.pallas_call(
        combine_kernel,
        out_shape=jax.ShapeDtypeStruct(blocks.shape, BF16),
        in_specs=[whole_vmem],
        out_specs=whole_vmem,
        compiler_params=pltpu.CompilerParams(vmem_limit_bytes=VMEM),
        cost_estimate=pl.CostEstimate(
            flops=20000000000, bytes_accessed=1000000, transcendentals=0
        ),
        name="combine",
    )(blocks)


def unpack_kernel(scale, position, own, other, grad_one, grad_two, sums):
    odd = position[0] % 2
    sums[pl.ds(pl.multiple_of(odd * HALF, HALF), HALF), :] = own[...]
    sums[pl.ds(pl.multiple_of((1 - odd) * HALF, HALF), HALF), :] = other[...]
    part = 3 * CH
    for a in range(3):
        for c in range(3):
            start = a * 3 * part + c * CH
            n = 9 * a + 3 * c

            def block(which):
                return sums[start + which * part : start + which * part + CH].astype(F32) * scale

            one, two, last = block(0), block(1).T, block(2)
            grad_one[n] = one[:, :CH]
            grad_one[n + 1] = one[:, CH:]
            grad_one[n + 2] = last[:, :CH]
            grad_two[26 - n] = two[:CH]
            grad_two[25 - n] = two[CH:]
            grad_two[24 - n] = last.T[CH:]


def unpack(scale, position, own, other):
    def kernel(*refs):
        unpack_kernel(scale, *refs)

    return pl.pallas_call(
        kernel,
        out_shape=(
            jax.ShapeDtypeStruct((27, CH, CH), F32),
            jax.ShapeDtypeStruct((27, CH, CH), F32),
        ),
        in_specs=[whole_smem, whole_vmem, whole_vmem],
        out_specs=(whole_vmem,) * 2,
        scratch_shapes=[pltpu.VMEM((TERMS, LANES), BF16)],
        compiler_params=pltpu.CompilerParams(vmem_limit_bytes=VMEM),
        name="unpack",
    )(position, own, other)


def near_swap(rows, devices):
    return lax.ppermute(rows, AXES, [(k, k ^ 1) for k in range(devices)])


def far_swap(rows, devices):
    route = [(k, k + 1) for k in range(1, devices - 1, 2)]
    route += [(k + 1, k) for k in range(1, devices - 1, 2)]
    return lax.ppermute(rows, AXES, route)


def local(devices, features, kernel_one, kernel_two, cotangent, neighbours, occupancy):
    position = lax.axis_index(AXES).astype(jnp.int32).reshape(1)
    near_send, far_send = pack(position, neighbours, features, cotangent, occupancy)
    near_send, far_send, later = lax.optimization_barrier((near_send, far_send, position))
    far = far_swap(far_send, devices)
    near = near_swap(near_send, devices)
    first, lookup, chosen, fields, spread = prepare(
        later, neighbours, kernel_one, kernel_two, features, cotangent, occupancy
    )
    result, given, kept = first_stage(
        lookup, chosen, occupancy, first, spread, near, far, fields
    )
    cores = [list(range(c, devices, 2)) for c in range(2)]
    blocks = devices // 2

    def to_all(rows):
        return lax.all_to_all(rows, AXES, 0, 0, axis_index_groups=cores, tiled=True)

    paired = pair_sum(kept, near_swap(given, devices))
    paired, later = lax.optimization_barrier((paired, later))
    terms = to_all(paired)
    second, near_send, far_send = relay(later, chosen, kernel_one, kernel_two, result)
    far = far_swap(far_send, devices)
    near = near_swap(near_send, devices)
    terms, second = lax.optimization_barrier((terms, second))
    output, grad_in = second_stage(lookup, occupancy, second, result, near, far)
    spread = combine(terms.reshape(blocks, HALF // blocks, LANES)).reshape(HALF, LANES)
    own = to_all(spread)
    own, output, grad_in = lax.optimization_barrier((own, output, grad_in))
    other = near_swap(own, devices)
    scale = float((SLOTS * VOX * devices) ** -0.5)
    grad_one, grad_two = unpack(scale, position, own, other)
    return output, grad_in, grad_one, grad_two


def solution(mesh):
    devices = mesh.shape["wide"] * mesh.shape["narrow"]
    bricks = P(AXES, None, None)
    in_specs = (bricks, P(), P(), bricks, P(AXES, None), P(AXES, None))
    out_specs = (bricks, bricks, P(), P())

    def run(*arrays):
        return local(devices, *arrays)

    return jax.shard_map(
        run, mesh=mesh, in_specs=in_specs, out_specs=out_specs, check_vma=False
    )
```

```python
import functools

import jax
import jax.numpy as jnp
from jax import lax
from jax.experimental import pallas as pl
from jax.experimental.pallas import tpu as pltpu
from jax.sharding import PartitionSpec as P

AXES = ("wide", "narrow")
SLOTS = 8
EDGE = 8
VOX = EDGE**3
CH = 64
LANES = 2 * CH
NEAR = 4
POOL = SLOTS + 2 * NEAR + 1
ZERO = POOL - 1
RIM = 304
SLAB = (EDGE + 2) * EDGE
TILE_ROWS = (EDGE + 2) * SLAB
ROWS = EDGE * SLAB
TERMS = 2048
HALF = TERMS // 2
VMEM = 24 * 1024 * 1024
F32 = jnp.float32
BF16 = jnp.bfloat16

whole_vmem = pl.BlockSpec(memory_space=pltpu.VMEM)
whole_smem = pl.BlockSpec(memory_space=pltpu.SMEM)
anywhere = pl.BlockSpec(memory_space=pl.ANY)


def lower_half(shape):
    return lax.broadcasted_iota(jnp.int32, shape, len(shape) - 1) < CH


def choose(index, neighbours, chosen):
    here = index * SLOTS
    odd = index % 2
    for r in range(SLOTS):
        chosen[0, r] = 0
        chosen[1, r] = 0
    count_ahead = jnp.int32(0)
    count_behind = jnp.int32(0)
    for b in range(SLOTS):
        highest = jnp.int32(-1)
        lowest = jnp.int32(1 << 20)
        for d in range(26):
            slot = neighbours[b, d]
            highest = jnp.maximum(highest, slot)
            lowest = jnp.minimum(lowest, jnp.where(slot < 0, 1 << 20, slot))
        chosen[odd, jnp.minimum(count_ahead, NEAR)] = b
        chosen[1 - odd, jnp.minimum(count_behind, NEAR)] = b
        count_ahead += (highest >= here + SLOTS).astype(jnp.int32)
        count_behind += (lowest < here).astype(jnp.int32)
    chosen[0, SLOTS - 1] = odd


def side_by_side(features, cotangent, occupancy, b):
    active = occupancy[pl.ds(b, 1), :].astype(F32)
    both = jnp.concatenate([features[b], cotangent[b]], axis=0).astype(F32) * active
    return both.T.astype(BF16)


def rim_rank(v):
    i, j, k = v >> 6, (v >> 3) & 7, v & 7
    inside = jnp.where(j == 0, k, jnp.where(j == 7, 20 + k, 6 + 2 * j + (k == 7).astype(jnp.int32)))
    inside = jnp.where((j == 0) | (j == 7) | (k == 0) | (k == 7), inside, RIM)
    return jnp.where(i == 0, v, jnp.where(i == 7, v - 216, 36 + 28 * i + inside))


def surface(v):
    i, j, k = v >> 6, (v >> 3) & 7, v & 7
    return (i == 0) | (i == 7) | (j == 0) | (j == 7) | (k == 0) | (k == 7)


def pack_kernel(
    narrow, neighbours_far, features_far, cotangent_far, occupancy_far,
    near_send, far_send, neighbours, features, cotangent, occupancy, sent, chosen, sems, out_sems,
):
    table = pltpu.make_async_copy(neighbours_far, neighbours, sems.at[5])
    table.start()
    loads = [pltpu.make_async_copy(occupancy_far, occupancy, sems.at[0])]
    for h in range(2):
        part = pl.ds(h * NEAR, NEAR)
        loads.append(
            pltpu.make_async_copy(features_far.at[part], features.at[part], sems.at[1 + h])
        )
        loads.append(
            pltpu.make_async_copy(cotangent_far.at[part], cotangent.at[part], sems.at[3 + h])
        )
    for copy in loads:
        copy.start()
    voxel = lax.broadcasted_iota(jnp.int32, (1, VOX), 1)
    rank = jnp.where(surface(voxel), rim_rank(voxel), -1)
    wanted = lax.broadcasted_iota(jnp.int32, (RIM, VOX), 0)
    select = jnp.where(rank == wanted, 1.0, 0.0).astype(BF16)
    table.wait()
    choose(lax.axis_index("wide") * narrow + lax.axis_index("narrow"), neighbours, chosen)
    stores = []
    for copy in loads:
        copy.wait()
    for side, target in ((1, far_send), (0, near_send)):
        for r in range(0, NEAR, 2):
            rows = []
            for q in range(2):
                b = chosen[side, r + q]
                active = occupancy[pl.ds(b, 1), :].astype(F32)
                rows.append((features[b].astype(F32) * active).astype(BF16))
                rows.append((cotangent[b].astype(F32) * active).astype(BF16))
            both = lax.dot_general(
                select,
                jnp.concatenate(rows, axis=0),
                (((1,), (1,)), ((), ())),
                preferred_element_type=F32,
            )
            for q in range(2):
                sent[side, r + q] = both[:, q * LANES : (q + 1) * LANES].astype(BF16)
            pair = pl.ds(r, 2)
            stores.append(
                pltpu.make_async_copy(
                    sent.at[side, pair], target.at[pair], out_sems.at[side, r // 2]
                )
            )
            stores[-1].start()
    for copy in stores:
        copy.wait()


def pack(narrow, neighbours, features, cotangent, occupancy):
    return pl.pallas_call(
        functools.partial(pack_kernel, narrow),
        out_shape=(
            jax.ShapeDtypeStruct((NEAR, RIM, LANES), BF16),
            jax.ShapeDtypeStruct((NEAR, RIM, LANES), BF16),
        ),
        in_specs=[anywhere] * 4,
        out_specs=(anywhere, anywhere),
        scratch_shapes=[
            pltpu.SMEM((SLOTS, 26), jnp.int32),
            pltpu.VMEM((SLOTS, CH, VOX), BF16),
            pltpu.VMEM((SLOTS, CH, VOX), BF16),
            pltpu.VMEM((SLOTS, VOX), jnp.int32),
            pltpu.VMEM((2, NEAR, RIM, LANES), BF16),
            pltpu.SMEM((2, SLOTS), jnp.int32),
            pltpu.SemaphoreType.DMA((6,)),
            pltpu.SemaphoreType.DMA((2, 2)),
        ],
        compiler_params=pltpu.CompilerParams(vmem_limit_bytes=60 * 1024 * 1024),
        name="pack",
    )(neighbours, features, cotangent, occupancy)


def weight_block(kernel, flip, a, rows, columns):
    def piece(c, e):
        if c is None or e is None:
            return jnp.zeros((CH, CH), F32)
        n = 9 * a + 3 * c + e
        return kernel[26 - n if flip else n].astype(F32)

    if flip:
        block = jnp.concatenate(
            [jnp.concatenate([piece(c, e) for c in columns], axis=1) for e in rows], axis=0
        )
    else:
        block = jnp.concatenate(
            [jnp.concatenate([piece(c, e) for e in rows], axis=1) for c in columns], axis=0
        ).T
    return block.astype(BF16)


def weight_field(kernel, flip, field, target):
    rows = ((0, 1), (2, None)) if field == 0 else ((None, 2), (0, 1))
    columns = ((0, 1), (2, None)) if field == 0 else ((1, 0), (None, 2))
    for a in range(3):
        for r in range(2):
            for s in range(2):
                target[
                    field, a, r * LANES : (r + 1) * LANES, s * LANES : (s + 1) * LANES
                ] = weight_block(kernel, flip, a, rows[r], columns[s])


def prepare_kernel(
    position, neighbours, kernel_one, kernel_two, features, cotangent, occupancy,
    first, lookup, chosen, fields, spread, flags, base,
):
    weight_field(kernel_one, False, 0, first)
    weight_field(kernel_two, True, 1, first)
    for b in range(SLOTS):
        fields[b] = side_by_side(features, cotangent, occupancy, b)
    choose(position[0], neighbours, chosen)
    voxel = lax.broadcasted_iota(jnp.int32, (VOX, LANES), 0)
    rank = jnp.where(surface(voxel), rim_rank(voxel), -1)
    for first_lane in range(0, RIM, LANES):
        count = min(LANES, RIM - first_lane)
        lane = lax.broadcasted_iota(jnp.int32, (VOX, LANES), 1) + first_lane
        block = jnp.where(rank == lane, 1.0, 0.0).astype(BF16)
        spread[:, first_lane : first_lane + count] = block[:, :count]
    start = (position[0] - 1) * SLOTS
    for s in range(3 * SLOTS + 1):
        flags[s] = 0
    for b in range(SLOTS):
        for d in range(26):
            slot = neighbours[b, d]
            flags[jnp.where(slot < 0, 3 * SLOTS, slot - start)] = 1
    odd = position[0] % 2
    count = jnp.int32(0)
    for s in range(SLOTS):
        base[s] = SLOTS + NEAR * (1 - odd) + jnp.minimum(count, NEAR - 1)
        count += flags[s]
        base[SLOTS + s] = s
    count = jnp.int32(0)
    for s in range(SLOTS):
        base[2 * SLOTS + s] = SLOTS + NEAR * odd + jnp.minimum(count, NEAR - 1)
        count += flags[2 * SLOTS + s]
    base[3 * SLOTS] = ZERO
    for b in range(SLOTS):
        lookup[b * 27 + 13] = b
        for d in range(26):
            slot = neighbours[b, d]
            lookup[b * 27 + d + (d > 12)] = base[jnp.where(slot < 0, 3 * SLOTS, slot - start)]


def prepare(position, neighbours, kernel_one, kernel_two, features, cotangent, occupancy):
    return pl.pallas_call(
        prepare_kernel,
        out_shape=(
            jax.ShapeDtypeStruct((2, 3, 2 * LANES, 2 * LANES), BF16),
            jax.ShapeDtypeStruct((27 * SLOTS,), jnp.int32),
            jax.ShapeDtypeStruct((2, SLOTS), jnp.int32),
            jax.ShapeDtypeStruct((SLOTS, VOX, LANES), BF16),
            jax.ShapeDtypeStruct((VOX, RIM), BF16),
        ),
        in_specs=[whole_smem, whole_smem] + [whole_vmem] * 5,
        out_specs=(whole_vmem, whole_smem, whole_smem) + (whole_vmem,) * 2,
        scratch_shapes=[pltpu.SMEM((32,), jnp.int32), pltpu.SMEM((32,), jnp.int32)],
        compiler_params=pltpu.CompilerParams(vmem_limit_bytes=VMEM),
        cost_estimate=pl.CostEstimate(flops=4000000, bytes_accessed=4000000, transcendentals=0),
        name="prepare",
    )(position, neighbours, kernel_one, kernel_two, features, cotangent, occupancy)


def relay_kernel(
    after, chosen, kernel_one, kernel_two, result, second, near_send, far_send
):
    for r in range(NEAR):
        far_send[r] = result[chosen[1, r]]
        near_send[r] = result[chosen[0, r]]
    weight_field(kernel_two, False, 0, second)
    weight_field(kernel_one, True, 1, second)


def relay(after, chosen, kernel_one, kernel_two, result):
    return pl.pallas_call(
        relay_kernel,
        out_shape=(
            jax.ShapeDtypeStruct((2, 3, 2 * LANES, 2 * LANES), BF16),
            jax.ShapeDtypeStruct((NEAR, VOX, LANES), BF16),
            jax.ShapeDtypeStruct((NEAR, VOX, LANES), BF16),
        ),
        in_specs=[whole_smem, whole_smem] + [whole_vmem] * 3,
        out_specs=(whole_vmem,) * 3,
        compiler_params=pltpu.CompilerParams(vmem_limit_bytes=VMEM),
        cost_estimate=pl.CostEstimate(
            flops=5000000000, bytes_accessed=2000000, transcendentals=0
        ),
        name="relay",
    )(after, chosen, kernel_one, kernel_two, result)


def fill_pool(own, before, after, pool, sems):
    copies = [
        pltpu.make_async_copy(own, pool.at[pl.ds(0, SLOTS)], sems.at[0]),
        pltpu.make_async_copy(before, pool.at[pl.ds(SLOTS, NEAR)], sems.at[1]),
        pltpu.make_async_copy(after, pool.at[pl.ds(SLOTS + NEAR, NEAR)], sems.at[2]),
    ]
    for copy in copies:
        copy.start()
    pool[ZERO] = jnp.zeros((VOX, LANES), BF16)
    for copy in copies:
        copy.wait()


def extend(pool, lookup, b, tile):
    def slabs(bricks, first, count):
        return [
            pool[brick, first : first + count, :].astype(F32).reshape(count // EDGE, EDGE, LANES)
            for brick in bricks
        ]

    for i in range(EDGE + 2):
        side = (i + EDGE - 1) // EDGE
        source = (i - 1) % EDGE
        bricks = [
            [lookup[b * 27 + side * 9 + j * 3 + k] for k in range(3)] for j in range(3)
        ]
        left = slabs(bricks[0], source * 64 + 48, 16)
        middle = slabs(bricks[1], source * 64, 64)
        right = slabs(bricks[2], source * 64, 16)
        low, centre, high = [
            jnp.concatenate([left[k][1:2], middle[k], right[k][0:1]], axis=0) for k in range(3)
        ]
        along = lax.broadcasted_iota(jnp.int32, centre.shape, 1)
        first = pltpu.roll(jnp.where(along == EDGE - 1, low, centre), 1, 1)
        last = pltpu.roll(jnp.where(along == 0, high, centre), EDGE - 1, 1)
        first, centre, last = [m.reshape(SLAB, LANES) for m in (first, centre, last)]
        lower = lower_half((SLAB, LANES))
        crossed = pltpu.roll(jnp.where(lower, centre, first), CH, 1)
        rows = pl.ds(i * SLAB, SLAB)
        tile[rows, 0:LANES] = jnp.where(lower, first, crossed).astype(BF16)
        tile[rows, LANES : 2 * LANES] = last.astype(BF16)
        tile[rows, 2 * LANES : 3 * LANES] = jnp.where(lower, crossed, centre).astype(BF16)


def convolve(tile, weights):
    sums = []
    for field in range(2):
        total = None
        for a in range(3):
            part = jnp.dot(
                tile[a * SLAB : a * SLAB + ROWS, field * LANES : (field + 2) * LANES],
                weights[field, a],
                preferred_element_type=F32,
            )
            total = part if total is None else total + part
        sums.append(total)

    def block(field, half):
        return sums[field][:, half * LANES : (half + 1) * LANES].reshape(
            EDGE, EDGE + 2, EDGE, LANES
        )

    zero, one = block(0, 0), block(1, 0)
    shape = (EDGE, EDGE, EDGE, LANES)
    lower = lower_half(shape)
    straight = jnp.where(lower, zero[:, 0:8], one[:, 0:8])
    crossed = jnp.where(lower, one[:, 1:9], zero[:, 1:9]).reshape(VOX, LANES)
    ends = block(0, 1)[:, 2:10] + block(1, 1)[:, 2:10]
    return (straight + ends).reshape(VOX, LANES) + pltpu.roll(crossed, CH, 1)


def row_mask(occupancy, b):
    active = occupancy[pl.ds(b, 1), :].astype(F32)
    return jnp.broadcast_to(active, (LANES, VOX)).T


def hidden_and_grad(both, mask):
    lower = lower_half((VOX, LANES))
    preact = jnp.where(lower, both, pltpu.roll(both, CH, 1))
    s = jax.nn.sigmoid(preact)
    value = jnp.where(lower, preact * s, both * s * (1.0 + preact * (1.0 - s)))
    return value * mask


def turned_over(value):
    cube = value.reshape(EDGE, EDGE, EDGE, LANES)
    turned = []
    for c in range(3):
        parts = [cube]
        if c > 0:
            parts.insert(0, jnp.zeros((EDGE, c, EDGE, LANES), F32))
        if c < 2:
            parts.append(jnp.zeros((EDGE, 2 - c, EDGE, LANES), F32))
        padded = jnp.concatenate(parts, axis=1).reshape(ROWS, LANES)
        turned.append(padded.astype(BF16).T)
    hidden = jnp.concatenate([t[:CH] for t in turned], axis=0)
    grad_pre = jnp.concatenate([t[CH:] for t in turned], axis=0)
    return hidden, grad_pre


def first_kernel(
    lookup, chosen, occupancy, weights, spread, near, far, own,
    result, given, kept, pool, tiles, sum_one, sum_two, terms, sems,
):
    load = pltpu.make_async_copy(own, pool.at[pl.ds(0, SLOTS)], sems.at[0])
    load.start()
    pool[ZERO] = jnp.zeros((VOX, LANES), BF16)
    for place, rim in ((SLOTS, near), (SLOTS + NEAR, far)):
        for r in range(0, NEAR, 2):
            whole = jnp.dot(
                spread[...],
                jnp.concatenate([rim[r], rim[r + 1]], axis=1),
                preferred_element_type=F32,
            )
            for q in range(2):
                pool[place + r + q] = whole[:, q * LANES : (q + 1) * LANES].astype(BF16)
    load.wait()
    sum_one[...] = jnp.zeros_like(sum_one)
    sum_two[...] = jnp.zeros_like(sum_two)
    group = 4

    @pl.loop(0, SLOTS // group)
    def _(t):
        turned = []
        for p in range(group):
            extend(pool, lookup, group * t + p, tiles.at[p])
        for p in range(group):
            b = group * t + p
            value = hidden_and_grad(convolve(tiles.at[p], weights), row_mask(occupancy, b))
            result[b] = value.astype(BF16)
            turned.append(turned_over(value))
        hidden = jnp.concatenate([h for h, _ in turned], axis=1)
        grad_pre = jnp.concatenate([g for _, g in turned], axis=1)
        for a in range(3):
            def rows(first):
                return jnp.concatenate(
                    [
                        tiles[p, a * SLAB : a * SLAB + ROWS, first : first + 2 * LANES]
                        for p in range(group)
                    ],
                    axis=0,
                )

            sum_one[a] += jnp.dot(grad_pre, rows(0), preferred_element_type=F32)
            sum_two[a] += jnp.dot(hidden, rows(LANES), preferred_element_type=F32)

    part = 3 * CH
    for a in range(3):
        start = a * 3 * part
        terms[start : start + part] = sum_one[a, :, 0:LANES]
        terms[start + part : start + 2 * part] = sum_two[a, :, LANES:]
        terms[start + 2 * part : start + 3 * part] = jnp.where(
            lower_half((part, LANES)), sum_one[a, :, LANES:], sum_two[a, :, 0:LANES]
        )
    terms[9 * part :] = jnp.zeros((TERMS - 9 * part, LANES), F32)
    odd = chosen[0, SLOTS - 1]
    given[...] = terms[pl.ds(pl.multiple_of((1 - odd) * HALF, HALF), HALF), :].astype(BF16)
    kept[...] = terms[pl.ds(pl.multiple_of(odd * HALF, HALF), HALF), :]


def first_stage(lookup, chosen, occupancy, weights, spread, near, far, own):
    return pl.pallas_call(
        first_kernel,
        out_shape=(
            jax.ShapeDtypeStruct((SLOTS, VOX, LANES), BF16),
            jax.ShapeDtypeStruct((HALF, LANES), BF16),
            jax.ShapeDtypeStruct((HALF, LANES), F32),
        ),
        in_specs=[whole_smem, whole_smem] + [whole_vmem] * 5 + [anywhere],
        out_specs=(whole_vmem,) * 3,
        scratch_shapes=[
            pltpu.VMEM((POOL, VOX, LANES), BF16),
            pltpu.VMEM((4, TILE_ROWS, 3 * LANES), BF16),
            pltpu.VMEM((3, 3 * CH, 2 * LANES), F32),
            pltpu.VMEM((3, 3 * CH, 2 * LANES), F32),
            pltpu.VMEM((TERMS, LANES), F32),
            pltpu.SemaphoreType.DMA((3,)),
        ],
        compiler_params=pltpu.CompilerParams(vmem_limit_bytes=VMEM),
        cost_estimate=pl.CostEstimate(
            flops=8000000000, bytes_accessed=6000000, transcendentals=600000
        ),
        name="first_stage",
    )(lookup, chosen, occupancy, weights, spread, near, far, own)


def second_kernel(
    lookup, occupancy, weights, own, before, after, output, grad_in, pool, tiles, sems
):
    fill_pool(own, before, after, pool, sems)
    group = 4

    @pl.loop(0, SLOTS // group)
    def _(t):
        for p in range(group):
            extend(pool, lookup, group * t + p, tiles.at[p])
        for p in range(group):
            b = group * t + p
            both = convolve(tiles.at[p], weights).T * occupancy[pl.ds(b, 1), :].astype(F32)
            output[b] = both[:CH].astype(BF16)
            grad_in[b] = both[CH:].astype(BF16)


def second_stage(lookup, occupancy, weights, own, before, after):
    return pl.pallas_call(
        second_kernel,
        out_shape=(
            jax.ShapeDtypeStruct((SLOTS, CH, VOX), BF16),
            jax.ShapeDtypeStruct((SLOTS, CH, VOX), BF16),
        ),
        in_specs=[whole_smem, whole_vmem, whole_vmem, anywhere, anywhere, anywhere],
        out_specs=(whole_vmem,) * 2,
        scratch_shapes=[
            pltpu.VMEM((POOL, VOX, LANES), BF16),
            pltpu.VMEM((4, TILE_ROWS, 3 * LANES), BF16),
            pltpu.SemaphoreType.DMA((3,)),
        ],
        compiler_params=pltpu.CompilerParams(vmem_limit_bytes=VMEM),
        cost_estimate=pl.CostEstimate(
            flops=8000000000, bytes_accessed=6000000, transcendentals=0
        ),
        name="second_stage",
    )(lookup, occupancy, weights, own, before, after)


def pair_kernel(kept, received, total):
    total[...] = (kept[...] + received[...].astype(F32)).astype(BF16)


def pair_sum(kept, received):
    return pl.pallas_call(
        pair_kernel,
        out_shape=jax.ShapeDtypeStruct((HALF, LANES), BF16),
        in_specs=[whole_vmem] * 2,
        out_specs=whole_vmem,
        compiler_params=pltpu.CompilerParams(vmem_limit_bytes=VMEM),
        name="pair_sum",
    )(kept, received)


def combine_kernel(blocks, spread):
    count, rows = blocks.shape[0], blocks.shape[1]
    total = jnp.zeros((rows, LANES), F32)
    for d in range(count):
        total += blocks[d].astype(F32)
    spread[...] = jnp.broadcast_to(total.astype(BF16)[None], spread.shape)


def combine(blocks):
    return pl.pallas_call(
        combine_kernel,
        out_shape=jax.ShapeDtypeStruct(blocks.shape, BF16),
        in_specs=[whole_vmem],
        out_specs=whole_vmem,
        compiler_params=pltpu.CompilerParams(vmem_limit_bytes=VMEM),
        cost_estimate=pl.CostEstimate(
            flops=20000000000, bytes_accessed=1000000, transcendentals=0
        ),
        name="combine",
    )(blocks)


def unpack_kernel(
    scale, position, own, other, one_far, two_far, sums, grad_one, grad_two, sems
):
    stores = []
    odd = position[0] % 2
    sums[pl.ds(pl.multiple_of(odd * HALF, HALF), HALF), :] = own[...]
    sums[pl.ds(pl.multiple_of((1 - odd) * HALF, HALF), HALF), :] = other[...]
    part = 3 * CH
    for a in range(3):
        for c in range(3):
            start = a * 3 * part + c * CH
            n = 9 * a + 3 * c

            def block(which):
                return sums[start + which * part : start + which * part + CH].astype(F32) * scale

            one, two, last = block(0), block(1).T, block(2)
            grad_one[n] = one[:, :CH]
            grad_one[n + 1] = one[:, CH:]
            grad_one[n + 2] = last[:, :CH]
            grad_two[26 - n] = two[:CH]
            grad_two[25 - n] = two[CH:]
            grad_two[24 - n] = last.T[CH:]
        for which, (source, target, first) in enumerate(
            ((grad_one, one_far, 9 * a), (grad_two, two_far, 18 - 9 * a))
        ):
            rows = pl.ds(first, 9)
            stores.append(
                pltpu.make_async_copy(source.at[rows], target.at[rows], sems.at[which, a])
            )
            stores[-1].start()
    for copy in stores:
        copy.wait()


def unpack(scale, position, own, other):
    def kernel(*refs):
        unpack_kernel(scale, *refs)

    return pl.pallas_call(
        kernel,
        out_shape=(
            jax.ShapeDtypeStruct((27, CH, CH), F32),
            jax.ShapeDtypeStruct((27, CH, CH), F32),
        ),
        in_specs=[whole_smem, whole_vmem, whole_vmem],
        out_specs=(anywhere, anywhere),
        scratch_shapes=[
            pltpu.VMEM((TERMS, LANES), BF16),
            pltpu.VMEM((27, CH, CH), F32),
            pltpu.VMEM((27, CH, CH), F32),
            pltpu.SemaphoreType.DMA((2, 3)),
        ],
        compiler_params=pltpu.CompilerParams(vmem_limit_bytes=VMEM),
        name="unpack",
    )(position, own, other)


def near_swap(rows, devices):
    return lax.ppermute(rows, AXES, [(k, k ^ 1) for k in range(devices)])


def far_swap(rows, devices):
    route = [(k, k + 1) for k in range(1, devices - 1, 2)]
    route += [(k + 1, k) for k in range(1, devices - 1, 2)]
    return lax.ppermute(rows, AXES, route)


def local(devices, narrow, features, kernel_one, kernel_two, cotangent, neighbours, occupancy):
    position = lax.axis_index(AXES).astype(jnp.int32).reshape(1)
    near_send, far_send = pack(narrow, neighbours, features, cotangent, occupancy)
    near_send, far_send, later = lax.optimization_barrier((near_send, far_send, position))
    far = far_swap(far_send, devices)
    near = near_swap(near_send, devices)
    first, lookup, chosen, fields, spread = prepare(
        later, neighbours, kernel_one, kernel_two, features, cotangent, occupancy
    )
    result, given, kept = first_stage(
        lookup, chosen, occupancy, first, spread, near, far, fields
    )
    cores = [list(range(c, devices, 2)) for c in range(2)]
    blocks = devices // 2

    def to_all(rows):
        return lax.all_to_all(rows, AXES, 0, 0, axis_index_groups=cores, tiled=True)

    paired = pair_sum(kept, near_swap(given, devices))
    paired, later = lax.optimization_barrier((paired, later))
    terms = to_all(paired)
    second, near_send, far_send = relay(later, chosen, kernel_one, kernel_two, result)
    far = far_swap(far_send, devices)
    near = near_swap(near_send, devices)
    terms, second = lax.optimization_barrier((terms, second))
    output, grad_in = second_stage(lookup, occupancy, second, result, near, far)
    spread = combine(terms.reshape(blocks, HALF // blocks, LANES)).reshape(HALF, LANES)
    own = to_all(spread)
    own, output, grad_in = lax.optimization_barrier((own, output, grad_in))
    other = near_swap(own, devices)
    scale = float((SLOTS * VOX * devices) ** -0.5)
    grad_one, grad_two = unpack(scale, position, own, other)
    return output, grad_in, grad_one, grad_two


def solution(mesh):
    devices = mesh.shape["wide"] * mesh.shape["narrow"]
    bricks = P(AXES, None, None)
    in_specs = (bricks, P(), P(), bricks, P(AXES, None), P(AXES, None))
    out_specs = (bricks, bricks, P(), P())

    def run(*arrays):
        return local(devices, mesh.shape["narrow"], *arrays)

    return jax.shard_map(
        run, mesh=mesh, in_specs=in_specs, out_specs=out_specs, check_vma=False
    )
```

```python
import functools

import jax
import jax.numpy as jnp
from jax import lax
from jax.experimental import pallas as pl
from jax.experimental.pallas import tpu as pltpu
from jax.sharding import PartitionSpec as P

AXES = ("wide", "narrow")
SLOTS = 8
EDGE = 8
VOX = EDGE**3
CH = 64
LANES = 2 * CH
NEAR = 4
POOL = SLOTS + 2 * NEAR + 1
ZERO = POOL - 1
RIM = 304
SLAB = (EDGE + 2) * EDGE
TILE_ROWS = (EDGE + 2) * SLAB
ROWS = EDGE * SLAB
TERMS = 2048
HALF = TERMS // 2
VMEM = 24 * 1024 * 1024
F32 = jnp.float32
BF16 = jnp.bfloat16

whole_vmem = pl.BlockSpec(memory_space=pltpu.VMEM)
whole_smem = pl.BlockSpec(memory_space=pltpu.SMEM)
anywhere = pl.BlockSpec(memory_space=pl.ANY)


def lower_half(shape):
    return lax.broadcasted_iota(jnp.int32, shape, len(shape) - 1) < CH


def choose(index, neighbours, chosen):
    here = index * SLOTS
    odd = index % 2
    for r in range(SLOTS):
        chosen[0, r] = 0
        chosen[1, r] = 0
    count_ahead = jnp.int32(0)
    count_behind = jnp.int32(0)
    for b in range(SLOTS):
        highest = jnp.int32(-1)
        lowest = jnp.int32(1 << 20)
        for d in range(26):
            slot = neighbours[b, d]
            highest = jnp.maximum(highest, slot)
            lowest = jnp.minimum(lowest, jnp.where(slot < 0, 1 << 20, slot))
        chosen[odd, jnp.minimum(count_ahead, NEAR)] = b
        chosen[1 - odd, jnp.minimum(count_behind, NEAR)] = b
        count_ahead += (highest >= here + SLOTS).astype(jnp.int32)
        count_behind += (lowest < here).astype(jnp.int32)
    chosen[0, SLOTS - 1] = odd


def side_by_side(features, cotangent, occupancy, b):
    active = occupancy[pl.ds(b, 1), :].astype(F32)
    both = jnp.concatenate([features[b], cotangent[b]], axis=0).astype(F32) * active
    return both.T.astype(BF16)


def rim_rank(v):
    i, j, k = v >> 6, (v >> 3) & 7, v & 7
    inside = jnp.where(j == 0, k, jnp.where(j == 7, 20 + k, 6 + 2 * j + (k == 7).astype(jnp.int32)))
    inside = jnp.where((j == 0) | (j == 7) | (k == 0) | (k == 7), inside, RIM)
    return jnp.where(i == 0, v, jnp.where(i == 7, v - 216, 36 + 28 * i + inside))


def surface(v):
    i, j, k = v >> 6, (v >> 3) & 7, v & 7
    return (i == 0) | (i == 7) | (j == 0) | (j == 7) | (k == 0) | (k == 7)


def pack_kernel(
    narrow, neighbours_far, features_far, cotangent_far, occupancy_far,
    near_send, far_send, neighbours, features, cotangent, occupancy, sent, chosen, sems, out_sems,
):
    table = pltpu.make_async_copy(neighbours_far, neighbours, sems.at[5])
    table.start()
    loads = [pltpu.make_async_copy(occupancy_far, occupancy, sems.at[0])]
    for h in range(2):
        part = pl.ds(h * NEAR, NEAR)
        loads.append(
            pltpu.make_async_copy(features_far.at[part], features.at[part], sems.at[1 + h])
        )
        loads.append(
            pltpu.make_async_copy(cotangent_far.at[part], cotangent.at[part], sems.at[3 + h])
        )
    for copy in loads:
        copy.start()
    voxel = lax.broadcasted_iota(jnp.int32, (1, VOX), 1)
    rank = jnp.where(surface(voxel), rim_rank(voxel), -1)
    wanted = lax.broadcasted_iota(jnp.int32, (RIM, VOX), 0)
    select = jnp.where(rank == wanted, 1.0, 0.0).astype(BF16)
    table.wait()
    choose(lax.axis_index("wide") * narrow + lax.axis_index("narrow"), neighbours, chosen)
    stores = []
    for copy in loads:
        copy.wait()
    for side, target in ((1, far_send), (0, near_send)):
        for r in range(0, NEAR, 2):
            rows = []
            for q in range(2):
                b = chosen[side, r + q]
                active = occupancy[pl.ds(b, 1), :].astype(F32)
                rows.append((features[b].astype(F32) * active).astype(BF16))
                rows.append((cotangent[b].astype(F32) * active).astype(BF16))
            both = lax.dot_general(
                select,
                jnp.concatenate(rows, axis=0),
                (((1,), (1,)), ((), ())),
                preferred_element_type=F32,
            )
            for q in range(2):
                sent[side, r + q] = both[:, q * LANES : (q + 1) * LANES].astype(BF16)
            pair = pl.ds(r, 2)
            stores.append(
                pltpu.make_async_copy(
                    sent.at[side, pair], target.at[pair], out_sems.at[side, r // 2]
                )
            )
            stores[-1].start()
    for copy in stores:
        copy.wait()


def pack(narrow, neighbours, features, cotangent, occupancy):
    return pl.pallas_call(
        functools.partial(pack_kernel, narrow),
        out_shape=(
            jax.ShapeDtypeStruct((NEAR, RIM, LANES), BF16),
            jax.ShapeDtypeStruct((NEAR, RIM, LANES), BF16),
        ),
        in_specs=[anywhere] * 4,
        out_specs=(anywhere, anywhere),
        scratch_shapes=[
            pltpu.SMEM((SLOTS, 26), jnp.int32),
            pltpu.VMEM((SLOTS, CH, VOX), BF16),
            pltpu.VMEM((SLOTS, CH, VOX), BF16),
            pltpu.VMEM((SLOTS, VOX), jnp.int32),
            pltpu.VMEM((2, NEAR, RIM, LANES), BF16),
            pltpu.SMEM((2, SLOTS), jnp.int32),
            pltpu.SemaphoreType.DMA((6,)),
            pltpu.SemaphoreType.DMA((2, 2)),
        ],
        compiler_params=pltpu.CompilerParams(vmem_limit_bytes=60 * 1024 * 1024),
        name="pack",
    )(neighbours, features, cotangent, occupancy)


def weight_block(kernel, flip, a, rows, columns):
    def piece(c, e):
        if c is None or e is None:
            return jnp.zeros((CH, CH), F32)
        n = 9 * a + 3 * c + e
        return kernel[26 - n if flip else n].astype(F32)

    if flip:
        block = jnp.concatenate(
            [jnp.concatenate([piece(c, e) for c in columns], axis=1) for e in rows], axis=0
        )
    else:
        block = jnp.concatenate(
            [jnp.concatenate([piece(c, e) for e in rows], axis=1) for c in columns], axis=0
        ).T
    return block.astype(BF16)


def weight_field(kernel, flip, field, target):
    rows = ((0, 1), (2, None)) if field == 0 else ((None, 2), (0, 1))
    columns = ((0, 1), (2, None)) if field == 0 else ((1, 0), (None, 2))
    for a in range(3):
        for r in range(2):
            for s in range(2):
                target[
                    field, a, r * LANES : (r + 1) * LANES, s * LANES : (s + 1) * LANES
                ] = weight_block(kernel, flip, a, rows[r], columns[s])


def prepare_kernel(
    position, neighbours, kernel_one, kernel_two, features, cotangent, occupancy,
    first, lookup, chosen, fields, spread, flags, base,
):
    weight_field(kernel_one, False, 0, first)
    weight_field(kernel_two, True, 1, first)
    for b in range(SLOTS):
        fields[b] = side_by_side(features, cotangent, occupancy, b)
    choose(position[0], neighbours, chosen)
    voxel = lax.broadcasted_iota(jnp.int32, (VOX, LANES), 0)
    rank = jnp.where(surface(voxel), rim_rank(voxel), -1)
    for first_lane in range(0, RIM, LANES):
        count = min(LANES, RIM - first_lane)
        lane = lax.broadcasted_iota(jnp.int32, (VOX, LANES), 1) + first_lane
        block = jnp.where(rank == lane, 1.0, 0.0).astype(BF16)
        spread[:, first_lane : first_lane + count] = block[:, :count]
    start = (position[0] - 1) * SLOTS
    for s in range(3 * SLOTS + 1):
        flags[s] = 0
    for b in range(SLOTS):
        for d in range(26):
            slot = neighbours[b, d]
            flags[jnp.where(slot < 0, 3 * SLOTS, slot - start)] = 1
    odd = position[0] % 2
    count = jnp.int32(0)
    for s in range(SLOTS):
        base[s] = SLOTS + NEAR * (1 - odd) + jnp.minimum(count, NEAR - 1)
        count += flags[s]
        base[SLOTS + s] = s
    count = jnp.int32(0)
    for s in range(SLOTS):
        base[2 * SLOTS + s] = SLOTS + NEAR * odd + jnp.minimum(count, NEAR - 1)
        count += flags[2 * SLOTS + s]
    base[3 * SLOTS] = ZERO
    for b in range(SLOTS):
        lookup[b * 27 + 13] = b
        for d in range(26):
            slot = neighbours[b, d]
            lookup[b * 27 + d + (d > 12)] = base[jnp.where(slot < 0, 3 * SLOTS, slot - start)]


def prepare(position, neighbours, kernel_one, kernel_two, features, cotangent, occupancy):
    return pl.pallas_call(
        prepare_kernel,
        out_shape=(
            jax.ShapeDtypeStruct((2, 3, 2 * LANES, 2 * LANES), BF16),
            jax.ShapeDtypeStruct((27 * SLOTS,), jnp.int32),
            jax.ShapeDtypeStruct((2, SLOTS), jnp.int32),
            jax.ShapeDtypeStruct((SLOTS, VOX, LANES), BF16),
            jax.ShapeDtypeStruct((VOX, RIM), BF16),
        ),
        in_specs=[whole_smem, whole_smem] + [whole_vmem] * 5,
        out_specs=(whole_vmem, whole_smem, whole_smem) + (whole_vmem,) * 2,
        scratch_shapes=[pltpu.SMEM((32,), jnp.int32), pltpu.SMEM((32,), jnp.int32)],
        compiler_params=pltpu.CompilerParams(vmem_limit_bytes=VMEM),
        cost_estimate=pl.CostEstimate(flops=4000000, bytes_accessed=4000000, transcendentals=0),
        name="prepare",
    )(position, neighbours, kernel_one, kernel_two, features, cotangent, occupancy)


def relay_kernel(
    after, chosen, kernel_one, kernel_two, result, second, near_send, far_send
):
    for r in range(NEAR):
        far_send[r] = result[chosen[1, r]]
        near_send[r] = result[chosen[0, r]]
    weight_field(kernel_two, False, 0, second)
    weight_field(kernel_one, True, 1, second)


def relay(after, chosen, kernel_one, kernel_two, result):
    return pl.pallas_call(
        relay_kernel,
        out_shape=(
            jax.ShapeDtypeStruct((2, 3, 2 * LANES, 2 * LANES), BF16),
            jax.ShapeDtypeStruct((NEAR, VOX, LANES), BF16),
            jax.ShapeDtypeStruct((NEAR, VOX, LANES), BF16),
        ),
        in_specs=[whole_smem, whole_smem] + [whole_vmem] * 3,
        out_specs=(whole_vmem,) * 3,
        compiler_params=pltpu.CompilerParams(vmem_limit_bytes=VMEM),
        cost_estimate=pl.CostEstimate(
            flops=5000000000, bytes_accessed=2000000, transcendentals=0
        ),
        name="relay",
    )(after, chosen, kernel_one, kernel_two, result)


def fill_pool(own, before, after, pool, sems):
    copies = [
        pltpu.make_async_copy(own, pool.at[pl.ds(0, SLOTS)], sems.at[0]),
        pltpu.make_async_copy(before, pool.at[pl.ds(SLOTS, NEAR)], sems.at[1]),
        pltpu.make_async_copy(after, pool.at[pl.ds(SLOTS + NEAR, NEAR)], sems.at[2]),
    ]
    for copy in copies:
        copy.start()
    pool[ZERO] = jnp.zeros((VOX, LANES), BF16)
    for copy in copies:
        copy.wait()


def extend(pool, lookup, b, tile):
    def slabs(bricks, first, count):
        return [
            pool[brick, first : first + count, :].astype(F32).reshape(count // EDGE, EDGE, LANES)
            for brick in bricks
        ]

    for i in range(EDGE + 2):
        side = (i + EDGE - 1) // EDGE
        source = (i - 1) % EDGE
        bricks = [
            [lookup[b * 27 + side * 9 + j * 3 + k] for k in range(3)] for j in range(3)
        ]
        left = slabs(bricks[0], source * 64 + 48, 16)
        middle = slabs(bricks[1], source * 64, 64)
        right = slabs(bricks[2], source * 64, 16)
        low, centre, high = [
            jnp.concatenate([left[k][1:2], middle[k], right[k][0:1]], axis=0) for k in range(3)
        ]
        along = lax.broadcasted_iota(jnp.int32, centre.shape, 1)
        first = pltpu.roll(jnp.where(along == EDGE - 1, low, centre), 1, 1)
        last = pltpu.roll(jnp.where(along == 0, high, centre), EDGE - 1, 1)
        first, centre, last = [m.reshape(SLAB, LANES) for m in (first, centre, last)]
        lower = lower_half((SLAB, LANES))
        crossed = pltpu.roll(jnp.where(lower, centre, first), CH, 1)
        rows = pl.ds(i * SLAB, SLAB)
        tile[rows, 0:LANES] = jnp.where(lower, first, crossed).astype(BF16)
        tile[rows, LANES : 2 * LANES] = last.astype(BF16)
        tile[rows, 2 * LANES : 3 * LANES] = jnp.where(lower, crossed, centre).astype(BF16)


def convolve(tile, weights):
    sums = []
    for field in range(2):
        total = None
        for a in range(3):
            part = jnp.dot(
                tile[a * SLAB : a * SLAB + ROWS, field * LANES : (field + 2) * LANES],
                weights[field, a],
                preferred_element_type=F32,
            )
            total = part if total is None else total + part
        sums.append(total)

    def block(field, half):
        return sums[field][:, half * LANES : (half + 1) * LANES].reshape(
            EDGE, EDGE + 2, EDGE, LANES
        )

    zero, one = block(0, 0), block(1, 0)
    shape = (EDGE, EDGE, EDGE, LANES)
    lower = lower_half(shape)
    straight = jnp.where(lower, zero[:, 0:8], one[:, 0:8])
    crossed = jnp.where(lower, one[:, 1:9], zero[:, 1:9]).reshape(VOX, LANES)
    ends = block(0, 1)[:, 2:10] + block(1, 1)[:, 2:10]
    return (straight + ends).reshape(VOX, LANES) + pltpu.roll(crossed, CH, 1)


def row_mask(occupancy, b):
    active = occupancy[pl.ds(b, 1), :].astype(F32)
    return jnp.broadcast_to(active, (LANES, VOX)).T


def hidden_and_grad(both, mask):
    lower = lower_half((VOX, LANES))
    preact = jnp.where(lower, both, pltpu.roll(both, CH, 1))
    s = jax.nn.sigmoid(preact)
    value = jnp.where(lower, preact * s, both * s * (1.0 + preact * (1.0 - s)))
    return value * mask


def turned_over(value):
    cube = value.reshape(EDGE, EDGE, EDGE, LANES)
    turned = []
    for c in range(3):
        parts = [cube]
        if c > 0:
            parts.insert(0, jnp.zeros((EDGE, c, EDGE, LANES), F32))
        if c < 2:
            parts.append(jnp.zeros((EDGE, 2 - c, EDGE, LANES), F32))
        padded = jnp.concatenate(parts, axis=1).reshape(ROWS, LANES)
        turned.append(padded.astype(BF16).T)
    hidden = jnp.concatenate([t[:CH] for t in turned], axis=0)
    grad_pre = jnp.concatenate([t[CH:] for t in turned], axis=0)
    return hidden, grad_pre


def first_kernel(
    lookup, chosen, occupancy, weights, spread, near, far, own,
    result, given, kept, pool, tiles, sum_one, sum_two, terms, sems,
):
    load = pltpu.make_async_copy(own, pool.at[pl.ds(0, SLOTS)], sems.at[0])
    load.start()
    pool[ZERO] = jnp.zeros((VOX, LANES), BF16)
    for place, rim in ((SLOTS, near), (SLOTS + NEAR, far)):
        for r in range(0, NEAR, 2):
            whole = jnp.dot(
                spread[...],
                jnp.concatenate([rim[r], rim[r + 1]], axis=1),
                preferred_element_type=F32,
            )
            for q in range(2):
                pool[place + r + q] = whole[:, q * LANES : (q + 1) * LANES].astype(BF16)
    load.wait()
    sum_one[...] = jnp.zeros_like(sum_one)
    sum_two[...] = jnp.zeros_like(sum_two)
    group = 4

    @pl.loop(0, SLOTS // group)
    def _(t):
        turned = []
        for p in range(group):
            extend(pool, lookup, group * t + p, tiles.at[p])
        for p in range(group):
            b = group * t + p
            value = hidden_and_grad(convolve(tiles.at[p], weights), row_mask(occupancy, b))
            result[b] = value.astype(BF16)
            turned.append(turned_over(value))
        hidden = jnp.concatenate([h for h, _ in turned], axis=1)
        grad_pre = jnp.concatenate([g for _, g in turned], axis=1)
        for a in range(3):
            def rows(first):
                return jnp.concatenate(
                    [
                        tiles[p, a * SLAB : a * SLAB + ROWS, first : first + 2 * LANES]
                        for p in range(group)
                    ],
                    axis=0,
                )

            sum_one[a] += jnp.dot(grad_pre, rows(0), preferred_element_type=F32)
            sum_two[a] += jnp.dot(hidden, rows(LANES), preferred_element_type=F32)

    part = 3 * CH
    for a in range(3):
        start = a * 3 * part
        terms[start : start + part] = sum_one[a, :, 0:LANES]
        terms[start + part : start + 2 * part] = sum_two[a, :, LANES:]
        terms[start + 2 * part : start + 3 * part] = jnp.where(
            lower_half((part, LANES)), sum_one[a, :, LANES:], sum_two[a, :, 0:LANES]
        )
    terms[9 * part :] = jnp.zeros((TERMS - 9 * part, LANES), F32)
    odd = chosen[0, SLOTS - 1]
    given[...] = terms[pl.ds(pl.multiple_of((1 - odd) * HALF, HALF), HALF), :].astype(BF16)
    kept[...] = terms[pl.ds(pl.multiple_of(odd * HALF, HALF), HALF), :]


def first_stage(lookup, chosen, occupancy, weights, spread, near, far, own):
    return pl.pallas_call(
        first_kernel,
        out_shape=(
            jax.ShapeDtypeStruct((SLOTS, VOX, LANES), BF16),
            jax.ShapeDtypeStruct((HALF, LANES), BF16),
            jax.ShapeDtypeStruct((HALF, LANES), F32),
        ),
        in_specs=[whole_smem, whole_smem] + [whole_vmem] * 5 + [anywhere],
        out_specs=(whole_vmem,) * 3,
        scratch_shapes=[
            pltpu.VMEM((POOL, VOX, LANES), BF16),
            pltpu.VMEM((4, TILE_ROWS, 3 * LANES), BF16),
            pltpu.VMEM((3, 3 * CH, 2 * LANES), F32),
            pltpu.VMEM((3, 3 * CH, 2 * LANES), F32),
            pltpu.VMEM((TERMS, LANES), F32),
            pltpu.SemaphoreType.DMA((3,)),
        ],
        compiler_params=pltpu.CompilerParams(vmem_limit_bytes=VMEM),
        cost_estimate=pl.CostEstimate(
            flops=8000000000, bytes_accessed=6000000, transcendentals=600000
        ),
        name="first_stage",
    )(lookup, chosen, occupancy, weights, spread, near, far, own)


def second_kernel(
    lookup, occupancy, weights, own, before, after, output, grad_in, pool, tiles, sems
):
    fill_pool(own, before, after, pool, sems)
    group = 4

    @pl.loop(0, SLOTS // group)
    def _(t):
        for p in range(group):
            extend(pool, lookup, group * t + p, tiles.at[p])
        for p in range(group):
            b = group * t + p
            both = convolve(tiles.at[p], weights).T * occupancy[pl.ds(b, 1), :].astype(F32)
            output[b] = both[:CH].astype(BF16)
            grad_in[b] = both[CH:].astype(BF16)


def second_stage(lookup, occupancy, weights, own, before, after):
    return pl.pallas_call(
        second_kernel,
        out_shape=(
            jax.ShapeDtypeStruct((SLOTS, CH, VOX), BF16),
            jax.ShapeDtypeStruct((SLOTS, CH, VOX), BF16),
        ),
        in_specs=[whole_smem, whole_vmem, whole_vmem, anywhere, anywhere, anywhere],
        out_specs=(whole_vmem,) * 2,
        scratch_shapes=[
            pltpu.VMEM((POOL, VOX, LANES), BF16),
            pltpu.VMEM((4, TILE_ROWS, 3 * LANES), BF16),
            pltpu.SemaphoreType.DMA((3,)),
        ],
        compiler_params=pltpu.CompilerParams(vmem_limit_bytes=VMEM),
        cost_estimate=pl.CostEstimate(
            flops=8000000000, bytes_accessed=6000000, transcendentals=0
        ),
        name="second_stage",
    )(lookup, occupancy, weights, own, before, after)


def pair_kernel(kept, received, total):
    total[...] = (kept[...] + received[...].astype(F32)).astype(BF16)


def pair_sum(kept, received):
    return pl.pallas_call(
        pair_kernel,
        out_shape=jax.ShapeDtypeStruct((HALF, LANES), BF16),
        in_specs=[whole_vmem] * 2,
        out_specs=whole_vmem,
        compiler_params=pltpu.CompilerParams(vmem_limit_bytes=VMEM),
        name="pair_sum",
    )(kept, received)


def combine_kernel(blocks, spread):
    count, rows = blocks.shape[0], blocks.shape[1]
    total = jnp.zeros((rows, LANES), F32)
    for d in range(count):
        total += blocks[d].astype(F32)
    spread[...] = jnp.broadcast_to(total.astype(BF16)[None], spread.shape)


def combine(blocks):
    return pl.pallas_call(
        combine_kernel,
        out_shape=jax.ShapeDtypeStruct(blocks.shape, BF16),
        in_specs=[whole_vmem],
        out_specs=whole_vmem,
        compiler_params=pltpu.CompilerParams(vmem_limit_bytes=VMEM),
        cost_estimate=pl.CostEstimate(
            flops=20000000000, bytes_accessed=1000000, transcendentals=0
        ),
        name="combine",
    )(blocks)


def unpack_kernel(
    scale, narrow, own, other, one_far, two_far, sums, grad_one, grad_two, sems
):
    stores = []
    odd = (lax.axis_index("wide") * narrow + lax.axis_index("narrow")) % 2
    sums[pl.ds(pl.multiple_of(odd * HALF, HALF), HALF), :] = own[...]
    sums[pl.ds(pl.multiple_of((1 - odd) * HALF, HALF), HALF), :] = other[...]
    part = 3 * CH
    for a in range(3):
        for c in range(3):
            start = a * 3 * part + c * CH
            n = 9 * a + 3 * c

            def block(which):
                return sums[start + which * part : start + which * part + CH].astype(F32) * scale

            one, two, last = block(0), block(1).T, block(2)
            grad_one[n] = one[:, :CH]
            grad_one[n + 1] = one[:, CH:]
            grad_one[n + 2] = last[:, :CH]
            grad_two[26 - n] = two[:CH]
            grad_two[25 - n] = two[CH:]
            grad_two[24 - n] = last.T[CH:]
        for which, (source, target, first) in enumerate(
            ((grad_one, one_far, 9 * a), (grad_two, two_far, 18 - 9 * a))
        ):
            rows = pl.ds(first, 9)
            stores.append(
                pltpu.make_async_copy(source.at[rows], target.at[rows], sems.at[which, a])
            )
            stores[-1].start()
    for copy in stores:
        copy.wait()


def unpack(scale, narrow, own, other):
    def kernel(*refs):
        unpack_kernel(scale, narrow, *refs)

    return pl.pallas_call(
        kernel,
        out_shape=(
            jax.ShapeDtypeStruct((27, CH, CH), F32),
            jax.ShapeDtypeStruct((27, CH, CH), F32),
        ),
        in_specs=[whole_vmem, whole_vmem],
        out_specs=(anywhere, anywhere),
        scratch_shapes=[
            pltpu.VMEM((TERMS, LANES), BF16),
            pltpu.VMEM((27, CH, CH), F32),
            pltpu.VMEM((27, CH, CH), F32),
            pltpu.SemaphoreType.DMA((2, 3)),
        ],
        compiler_params=pltpu.CompilerParams(vmem_limit_bytes=VMEM),
        name="unpack",
    )(own, other)


def near_swap(rows, devices):
    return lax.ppermute(rows, AXES, [(k, k ^ 1) for k in range(devices)])


def far_swap(rows, devices):
    route = [(k, k + 1) for k in range(1, devices - 1, 2)]
    route += [(k + 1, k) for k in range(1, devices - 1, 2)]
    return lax.ppermute(rows, AXES, route)


def local(devices, narrow, features, kernel_one, kernel_two, cotangent, neighbours, occupancy):
    position = lax.axis_index(AXES).astype(jnp.int32).reshape(1)
    near_send, far_send = pack(narrow, neighbours, features, cotangent, occupancy)
    near_send, far_send, later = lax.optimization_barrier((near_send, far_send, position))
    far = far_swap(far_send, devices)
    near = near_swap(near_send, devices)
    first, lookup, chosen, fields, spread = prepare(
        later, neighbours, kernel_one, kernel_two, features, cotangent, occupancy
    )
    result, given, kept = first_stage(
        lookup, chosen, occupancy, first, spread, near, far, fields
    )
    cores = [list(range(c, devices, 2)) for c in range(2)]
    blocks = devices // 2

    def to_all(rows):
        return lax.all_to_all(rows, AXES, 0, 0, axis_index_groups=cores, tiled=True)

    paired = pair_sum(kept, near_swap(given, devices))
    paired, later = lax.optimization_barrier((paired, later))
    terms = to_all(paired)
    second, near_send, far_send = relay(later, chosen, kernel_one, kernel_two, result)
    far = far_swap(far_send, devices)
    near = near_swap(near_send, devices)
    terms, second = lax.optimization_barrier((terms, second))
    output, grad_in = second_stage(lookup, occupancy, second, result, near, far)
    spread = combine(terms.reshape(blocks, HALF // blocks, LANES)).reshape(HALF, LANES)
    own = to_all(spread)
    own, output, grad_in = lax.optimization_barrier((own, output, grad_in))
    other = near_swap(own, devices)
    scale = float((SLOTS * VOX * devices) ** -0.5)
    grad_one, grad_two = unpack(scale, narrow, own, other)
    return output, grad_in, grad_one, grad_two


def solution(mesh):
    devices = mesh.shape["wide"] * mesh.shape["narrow"]
    bricks = P(AXES, None, None)
    in_specs = (bricks, P(), P(), bricks, P(AXES, None), P(AXES, None))
    out_specs = (bricks, bricks, P(), P())

    def run(*arrays):
        return local(devices, mesh.shape["narrow"], *arrays)

    return jax.shard_map(
        run, mesh=mesh, in_specs=in_specs, out_specs=out_specs, check_vma=False
    )
```
